128 devices in a mesh: dp: 8 (over x, core), ctx: 16 (over y, z).
Axes of the slice: x: 4, y: 4, z: 4, core: 2. Of those that a mesh axis runs over, the one named last changes fastest.
Arguments:
- layer_input: bfloat16 [16384, 6144], P(('dp', 'ctx')), may hold values from -24 to 24
- query_rows: bfloat16 [16384, 4096], P(('dp', 'ctx')), may hold values from -5 to 5
- key_rows: bfloat16 [16384, 4096], P(('dp', 'ctx')), may hold values from -5 to 5
- value_rows: bfloat16 [16384, 4096], P(('dp', 'ctx')), may hold values from -6 to 6
- out_grad: bfloat16 [16384, 4096], P(('dp', 'ctx')), may hold values from -6 to 6
- doc_lengths: int32 [8, 16], P('dp'), may hold values from 1 to 1024, 2048 in all within a row
- dilations: int32 [16], replicated, may hold values from 2 to 8, as said below
- seg_lengths: int32 [16], replicated, may hold values from 256 to 2048, as said below
Outputs:
- attention_out: bfloat16 [16384, 4096], P(('dp', 'ctx'))
- grad_query: bfloat16 [16384, 4096], P(('dp', 'ctx'))
- grad_key: bfloat16 [16384, 4096], P(('dp', 'ctx'))
- grad_value: bfloat16 [16384, 4096], P(('dp', 'ctx'))
- weight_grad: float32 [6144, 3, 4096], P('dp', None, 'ctx')
The draws below stay inside these ranges and needn't reach their ends.
Inputs may be any that keep to these rules, and one draw needn't show every extreme that they name: `dilations`: each rate is 2, 4 or 8; in every draw some head group has rate 2. `seg_lengths`: each segment length is 2048 divided by 1, 2, 4 or 8.
All inputs are finite; a program needn't handle non-finite values.
Results may differ from the reference program's by a relative error of at most 0.015.
Values may be sent and summed in bfloat16 or wider, within the bound.
A program may use at most 128 MiB of HBM per device.

```python
import math
import jax
import jax.numpy as jnp
import numpy as np
from jax import lax

D = 6144
HEADS = 32
HS = 128
GROUPS = 16
DOCS = 16
LEN = 2048
TOKENS = 16384
N_DP = 8


def draw_query_rows(key, part):
    key = jax.random.fold_in(key, 1)
    return jax.random.truncated_normal(key, -5.0, 5.0, (TOKENS, HEADS * HS), jnp.float32).astype(jnp.bfloat16)


def draw_key_rows(key, part):
    key = jax.random.fold_in(key, 2)
    return jax.random.truncated_normal(key, -5.0, 5.0, (TOKENS, HEADS * HS), jnp.float32).astype(jnp.bfloat16)


def draw_dilations(key, part):
    key = jax.random.fold_in(key, 3)
    power_key, chosen_key = jax.random.split(key)
    powers = jax.random.randint(power_key, (GROUPS,), 1, 4)
    chosen = jax.random.randint(chosen_key, (), 0, GROUPS)
    picked = jnp.power(2, powers)
    return jnp.where(jnp.arange(GROUPS) == chosen, 2, picked).astype(jnp.int32)


def draw_seg_lengths(key, part):
    key = jax.random.fold_in(key, 4)
    powers = jax.random.randint(key, (GROUPS,), 0, 4)
    return (LEN // jnp.power(2, powers)).astype(jnp.int32)


def with_spikes(values, stream_key, source, target, parts, factor):
    owner, partner = [(jnp.arange(values.shape[dim]) // (values.shape[dim] // parts)).reshape([-1 if axis == dim else 1 for axis in range(values.ndim)]) for dim in (source, target)]
    chosen = jax.random.permutation(stream_key, parts)[partner]
    strong = (owner == chosen) | (owner == (partner + parts // 2) % parts)
    return jnp.where(strong, factor * values, values)


def block_scale(own_key, extent, pieces, low, largest):
    loudness, own = 1.0, jax.random.fold_in(own_key, 6)
    for axis_at, shards_of in pieces:
        steps = jnp.exp(jax.random.uniform(jax.random.fold_in(own, axis_at), (shards_of,), jnp.float32, low / len(pieces), largest / len(pieces)))
        loudness = loudness * jnp.repeat(steps, extent[axis_at] // shards_of).reshape([-1 if axis == axis_at else 1 for axis in range(len(extent))])
    return loudness


def profile(amount, total, limit, lean):
    loads = [(1 << 20) // math.isqrt(standing ** lean) + 1 for standing in range(2, amount + 1)]
    surplus, holding = total - limit - (amount - 1), [1] * (amount - 1)
    while surplus > 0:
        free = [i for i in range(amount - 1) if holding[i] < limit]
        pool, budget = sum([loads[i] for i in free]), surplus
        for i in free:
            addition = min(limit - holding[i], max(1, budget * loads[i] // pool), surplus)
            holding[i] = holding[i] + addition
            surplus = surplus - addition
    return np.array([limit] + holding)


def uneven(stream_key, count, total, reach, lean):
    if count == 2:
        one = jax.random.randint(stream_key, (), max(1, total - reach), min(reach, total - 1) + 1)
        return jnp.stack([one, total - one])
    lengths = jnp.asarray(profile(count, total, reach, lean), jnp.int32)
    pairs = (count - 1) // 2
    source_of, taker = lengths[1:1 + 2 * pairs:2], lengths[2:2 + 2 * pairs:2]
    margin = jnp.minimum(source_of - 1, reach - taker)
    passed = jax.random.randint(jax.random.fold_in(stream_key, 1), (pairs,), 0, 1 << 20) % (margin + 1)
    lengths = lengths.at[1:1 + 2 * pairs:2].set(source_of - passed).at[2:2 + 2 * pairs:2].set(taker + passed)
    return lengths[jax.random.permutation(jax.random.fold_in(stream_key, 2), count)]


def bell_draw(key, shape, scale, bound, cuts=(), kind=jnp.bfloat16):
    values = jax.random.normal(key, shape, jnp.float32) * scale
    if len(cuts) > 0:
        values = block_scale(key, shape, cuts, -0.22, 0.18) * values
    return jnp.clip(values, min=-bound, max=bound).astype(kind)


def gaussian_with(own_key, shape, deviation, bound, cuts, heavy, held_as=jnp.bfloat16):
    drawn = deviation * jax.random.normal(own_key, shape, jnp.float32)
    if cuts:
        drawn = drawn * block_scale(own_key, shape, cuts, -0.22, 0.18)
    return jnp.clip(with_spikes(drawn, jax.random.fold_in(own_key, 3), *heavy), -bound, bound).astype(held_as)


def setup_inputs(seed: int = 0) -> dict:
    key_list = jax.random.split(jax.random.key(seed), 9)
    layer_input = gaussian_with(key_list[0], (TOKENS, D), 1.0, 24.0, ((0, 128),), (0, 1, 128, 5.5))
    query_rows = draw_query_rows(jax.random.fold_in(key_list[8], 71), 0)
    key_rows = draw_key_rows(jax.random.fold_in(key_list[8], 71), 0)
    value_rows = bell_draw(key_list[3], (TOKENS, HEADS * HS), 1.0, 6.0, ((0, 128),))
    out_grad = bell_draw(key_list[4], (TOKENS, HEADS * HS), 1.0, 6.0, ((0, 128),))
    doc_lengths = jax.vmap(lambda own: uneven(own, DOCS, LEN, LEN // 2, 2))(jax.random.split(key_list[5], N_DP)).reshape((N_DP, DOCS)).astype(jnp.int32)
    dilations = draw_dilations(jax.random.fold_in(key_list[8], 71), 0)
    seg_lengths = draw_seg_lengths(jax.random.fold_in(key_list[8], 71), 0)
    return dict(layer_input=layer_input, query_rows=query_rows, key_rows=key_rows, value_rows=value_rows, out_grad=out_grad, doc_lengths=doc_lengths, dilations=dilations, seg_lengths=seg_lengths)


def doc_of(lengths_row, positions):
    doc_ends = jnp.cumsum(lengths_row, dtype=jnp.int32)
    return lax.optimization_barrier(jnp.sum((positions[:, None] >= doc_ends[None, :]).astype(jnp.int32), axis=1))

def attend(queries, keys, values, cotangent, position, usable, doc_id, segment):
    highest = lax.Precision.HIGHEST
    count = position.shape[0]
    slot_ids = jnp.arange(count, dtype=jnp.int32)
    allowed = usable[:, None] & usable[None, :] & (doc_id[:, None] == doc_id[None, :]) & (segment[:, None] == segment[None, :]) & (position[None, :] <= position[:, None])
    allowed = allowed | (slot_ids[:, None] == slot_ids[None, :])
    score_scale = 1.0 / math.sqrt(HS)
    scores = jnp.einsum('qhd,khd->hqk', queries, keys, precision=highest) * score_scale
    scores = jnp.where(allowed[None], scores, -1e+30)
    row_max = lax.optimization_barrier(jnp.max(scores, axis=2, keepdims=True))
    expos = jnp.exp(scores - row_max)
    probs = expos / lax.optimization_barrier(jnp.sum(expos, axis=2, keepdims=True))
    weights = lax.optimization_barrier(probs.astype(jnp.bfloat16)).astype(jnp.float32)
    result = jnp.einsum('hqk,khd->qhd', weights, values, precision=highest).astype(jnp.bfloat16)
    dprob = jnp.einsum('qhd,khd->hqk', cotangent, values, precision=highest)
    delta = lax.optimization_barrier(jnp.sum(probs * dprob, axis=2, keepdims=True))
    dscore = lax.optimization_barrier((probs * (dprob - delta) * score_scale).astype(jnp.bfloat16)).astype(jnp.float32)
    grad_q = jnp.einsum('hqk,khd->qhd', dscore, keys, precision=highest).astype(jnp.bfloat16)
    grad_k = jnp.einsum('hqk,qhd->khd', dscore, queries, precision=highest).astype(jnp.bfloat16)
    grad_v = jnp.einsum('hqk,qhd->khd', weights, cotangent, precision=highest).astype(jnp.bfloat16)
    return (result, grad_q, grad_k, grad_v)

def reference(layer_input, query_rows, key_rows, value_rows, out_grad, doc_lengths, dilations, seg_lengths):
    highest = lax.Precision.HIGHEST
    width = query_rows.shape[1]
    groups = dilations.shape[0]
    group_width = width // groups
    half = LEN // 2
    slot = jnp.arange(half, dtype=jnp.int32)
    grad_scale = 1.0 / math.sqrt(TOKENS)
    summed = jnp.zeros((groups, D, 3, group_width), jnp.float32)
    results = [[], [], [], []]
    for pack in range(N_DP):
        first = pack * LEN
        pack_input = layer_input[first:first + LEN]
        pack_arrays = [query_rows[first:first + LEN], key_rows[first:first + LEN], value_rows[first:first + LEN], out_grad[first:first + LEN]]
        lengths_row = doc_lengths[pack]

        def one_group(group):
            rate = dilations[group]
            offset = group % rate
            position = offset + rate * slot
            usable = slot < LEN // rate
            rows_safe = jnp.where(usable, position, 0).astype(jnp.int32)

            def pick(tensor):
                columns = lax.dynamic_slice_in_dim(tensor, group * group_width, group_width, 1)
                taken = jnp.take(columns, rows_safe, axis=0)
                taken = jnp.where(usable[:, None], taken, jnp.zeros_like(taken))
                return taken.astype(jnp.float32).reshape(half, group_width // HS, HS)
            picked = [pick(tensor) for tensor in pack_arrays]
            input_taken = jnp.take(pack_input, rows_safe, axis=0)
            input_taken = jnp.where(usable[:, None], input_taken, jnp.zeros_like(input_taken)).astype(jnp.float32)
            doc_id = doc_of(lengths_row, position)
            segment = position // seg_lengths[group]
            result, grad_q, grad_k, grad_v = attend(picked[0], picked[1], picked[2], picked[3], position, usable, doc_id, segment)
            stacked = jnp.stack([grad_q, grad_k, grad_v], axis=1).astype(jnp.float32).reshape(half, 3, group_width)
            term = jnp.einsum('sd,stc->dtc', input_taken, stacked, precision=highest) * grad_scale
            term = lax.optimization_barrier(term.astype(jnp.bfloat16)).astype(jnp.float32)
            home = jnp.where(usable, position, LEN).astype(jnp.int32)

            def place(tensor):
                return jnp.zeros((LEN + 1, group_width), jnp.bfloat16).at[home].set(tensor.reshape(half, group_width))[:LEN]
            return (place(result), place(grad_q), place(grad_k), place(grad_v), term)
        placed_out, placed_q, placed_k, placed_v, term = lax.map(one_group, jnp.arange(groups, dtype=jnp.int32))
        summed = summed + term
        for index, placed in enumerate((placed_out, placed_q, placed_k, placed_v)):
            results[index].append(jnp.transpose(placed, (1, 0, 2)).reshape(LEN, width))
    weight_grad = jnp.transpose(summed, (1, 2, 0, 3)).reshape(D, 3, width)
    return (jnp.concatenate(results[0], axis=0), jnp.concatenate(results[1], axis=0), jnp.concatenate(results[2], axis=0), jnp.concatenate(results[3], axis=0), weight_grad)
```

```python
import functools
import math

import jax
import jax.numpy as jnp
from jax import lax
from jax.experimental import pallas as pl
from jax.experimental.pallas import tpu as pltpu
from jax.sharding import PartitionSpec as P

MESH = pl.DeviceIdType.MESH
HS = 128
SIDE = 4
CTX = 16
ROWS = 128
HALF = 64
SLOTS = 1024
GW = 256
D = 6144
BLOCK = 768
CHUNKS = 4
BQ = 256
BF = jnp.bfloat16
F32 = jnp.float32
OFFSETS = (
    (0, 1), (1, 0), (0, 3), (3, 0), (1, 1), (3, 3), (1, 3), (3, 1),
    (0, 2), (2, 0), (1, 2), (2, 1), (3, 2), (2, 3), (2, 2),
)


def nt(a, b):
    return lax.dot_general(a, b, (((1,), (1,)), ((), ())), preferred_element_type=F32)


def nn(a, b):
    return jnp.dot(a, b, preferred_element_type=F32)


def slot_ids(shape, dim, parity, group, lengths, rate, seg_len):
    pos = 2 * lax.broadcasted_iota(jnp.int32, shape, dim) + parity
    doc = jnp.zeros(shape, jnp.int32)
    end = jnp.int32(0)
    for d in range(16):
        end = end + lengths[0, d]
        doc = doc + (pos >= end).astype(jnp.int32)
    seg = jnp.zeros(shape, jnp.int32)
    for m in range(1, 8):
        seg = seg + (pos >= m * seg_len).astype(jnp.int32)
    usable = ((pos - group) & (rate - 1)) == 0
    return doc * 8 + seg, usable


def kernel(
    x_hbm, q_hbm, k_hbm, v_hbm, g_hbm, lengths, rates, segs,
    back, wsum,
    x_in, t_in, sq, rq, xo, xg, yb, gt, idk_ref, idq_ref, use_ref, kt, vt, gk_acc, gv_acc,
    pb, sib, rbuf, rel, rx,
    load_sem, loc_sem, bar_free, a_ss, a_rs, b_ss, b_rs, x_ss, x_rs, w_ss, w_rs,
):
    del bar_free
    dp = lax.axis_index("dp")
    me = lax.axis_index("ctx")
    xx, core = dp // 2, dp % 2
    yy, zz = me // SIDE, me % SIDE
    parity = zz % 2

    def at(dy, dz):
        return ((yy + dy) % SIDE) * SIDE + (zz + dz) % SIDE

    def at_x(dx):
        return ((xx + dx) % 4) * 2 + core

    loads = [
        pltpu.make_async_copy(src, t_in.at[i], load_sem.at[i])
        for i, src in enumerate((q_hbm, k_hbm, v_hbm, g_hbm))
    ]
    loads.append(pltpu.make_async_copy(x_hbm, x_in, load_sem.at[4]))
    for load in loads:
        load.start()

    barrier = pltpu.get_barrier_semaphore()
    peers = [(dp, at(dy, dz)) for dy, dz in OFFSETS]
    peers += [(xx * 2 + 1 - core, me), (at_x(1), me), (at_x(3), me)]
    for peer in peers:
        pl.semaphore_signal(barrier, inc=1, device_id=peer, device_id_type=MESH)
    pl.semaphore_wait(barrier, len(peers))

    pending = []

    def send(src, dst, ss, rs, peer):
        copy = pltpu.make_async_remote_copy(
            src_ref=src, dst_ref=dst, send_sem=ss, recv_sem=rs, device_id=peer, device_id_type=MESH
        )
        copy.start()
        return copy

    for load in loads[:4]:
        load.wait()
    row = lax.broadcasted_iota(jnp.int32, (HALF, ROWS), 0)
    col = lax.broadcasted_iota(jnp.int32, (HALF, ROWS), 1)
    picks = [(col == 2 * row + par).astype(F32).astype(BF) for par in range(2)]

    def gather_group(pair, carry):
        for par in range(2):
            group = 2 * pair + par
            cols = pl.ds(pl.multiple_of(group * GW, GW), GW)
            for t in range(4):
                sq[group, t] = nn(picks[par], t_in[t, :, cols]).astype(BF)
        return carry

    lax.fori_loop(0, CTX // 2, gather_group, 0)
    own_q = pltpu.make_async_copy(sq.at[me], rq.at[me], loc_sem.at[0])
    own_q.start()
    out_q = [
        send(sq.at[at(dy, dz)], rq.at[me], a_ss.at[i], a_rs.at[i], (dp, at(dy, dz)))
        for i, (dy, dz) in enumerate(OFFSETS)
    ]

    loads[4].wait()
    row2 = lax.broadcasted_iota(jnp.int32, (ROWS, ROWS), 0)
    col2 = lax.broadcasted_iota(jnp.int32, (ROWS, ROWS), 1)
    wanted = jnp.where(row2 < HALF, 2 * row2 + parity, 2 * (row2 - HALF) + 1 - parity)
    permute = (col2 == wanted).astype(F32).astype(BF)
    targets = [(xx + 2) % 4, (xx + 1) % 4, (xx + 3) % 4, xx]
    stage = [dict() for _ in range(CHUNKS)]

    def xsend(k, name, i, src, dst, dy, dz):
        stage[k][name] = send(src, dst, x_ss.at[k, i], x_rs.at[k, i], (dp, at(dy, dz)))

    def first(k):
        base = targets[k] * (2 * BLOCK)
        for part in range(2):
            for n in range(3):
                cols = pl.ds(pl.multiple_of(base + part * BLOCK + n * 256, 256), 256)
                here = slice(n * 256, (n + 1) * 256)
                both = nn(permute, x_in[:, cols]).astype(BF)
                if part == 0:
                    xg[k, 0, yy, zz, :, here] = both[:HALF]
                    xo[k, :, here] = both[HALF:]
                else:
                    yb[k, 0, yy, :, here] = both[:HALF]
                    yb[k, 1, yy, :, here] = both[HALF:]
        home = xg.at[k, 0, yy, zz]
        xsend(k, "a1p", 0, xo.at[k], home, 0, 1)
        xsend(k, "a1m", 1, xo.at[k], home, 0, 3)
        xsend(k, "b1p", 3, yb.at[k, :, yy], yb.at[k, :, yy], 1, 0)
        xsend(k, "b1m", 4, yb.at[k, :, yy], yb.at[k, :, yy], 3, 0)
        xsend(k, "a12", 2, home, home, 0, 2)

    def second(k):
        stage[k]["a1p"].wait_recv()
        stage[k]["a1m"].wait_recv()
        stage[k]["a12"].wait_recv()
        mine = xg.at[k, 0, yy]
        xsend(k, "a2p", 5, mine, mine, 1, 0)
        xsend(k, "a2m", 6, mine, mine, 3, 0)
        stage[k]["b1p"].wait_recv()
        below = yb.at[k, 0, (yy + 3) % SIDE]
        xsend(k, "b2p", 7, below, below, 1, 0)
        stage[k]["b1m"].wait_recv()
        above = yb.at[k, 1, (yy + 1) % SIDE]
        xsend(k, "b2m", 8, above, above, 3, 0)

    def third(k):
        stage[k]["b2p"].wait_recv()
        stage[k]["b2m"].wait_recv()
        there = xg.at[k, 1, :, zz]
        xsend(k, "b3p", 9, yb.at[k, 1], there, 0, 1)
        xsend(k, "b3m", 10, yb.at[k, 1], there, 0, 3)
        xsend(k, "b32", 11, yb.at[k, 0], there, 0, 2)
        local = pltpu.make_async_copy(yb.at[k, 0], there, loc_sem.at[1 + k])
        local.start()
        stage[k]["local"] = local
        stage[k]["a2p"].wait_recv()
        below = xg.at[k, 0, (yy + 3) % SIDE, 0:2]
        xsend(k, "a3p", 12, below, below, 1, 0)
        stage[k]["a2m"].wait_recv()
        above = xg.at[k, 0, (yy + 1) % SIDE, 2:4]
        xsend(k, "a3m", 13, above, above, 3, 0)

    def arrived(k):
        stage[k].pop("local").wait()
        for name in ("a3p", "a3m", "b3p", "b3m", "b32"):
            stage[k][name].wait_recv()

    for k in range(CHUNKS):
        first(k)

    rate, seg_len = rates[me], segs[me]
    ids, usable = slot_ids((SLOTS, 1), 0, parity, me, lengths, rate, seg_len)
    idk_ref[...] = jnp.where(usable, ids, -1)
    ids, usable = slot_ids((1, SLOTS), 1, parity, me, lengths, rate, seg_len)
    idq_ref[...] = jnp.where(usable, ids, -2)
    use_ref[...] = usable.astype(F32)

    second(0)
    second(1)
    own_q.wait()
    for copy in out_q:
        copy.wait_recv()
    for copy in out_q:
        copy.wait_send()

    scale = 1.0 / math.sqrt(HS)
    log2e = 1.4426950408889634

    def heads(h, t, count):
        return rq[0:count, t, :, h * HS:(h + 1) * HS].reshape(count * HALF, HS)

    def attend(h, i):
        count = (i + 1) * (BQ // HALF)
        w = (i + 1) * BQ
        mine = slice(i * (BQ // HALF), (i + 1) * (BQ // HALF))
        cols = slice(h * HS, (h + 1) * HS)
        q = rq[mine, 0, :, cols].reshape(BQ, HS)
        g = rq[mine, 3, :, cols].reshape(BQ, HS)
        queries = slice(i * BQ, (i + 1) * BQ)
        idq = idq_ref[:, queries]
        allowed = (idk_ref[0:w] == idq) & (
            lax.broadcasted_iota(jnp.int32, (w, BQ), 0)
            <= lax.broadcasted_iota(jnp.int32, (w, BQ), 1) + i * BQ
        )
        s = jnp.where(allowed, nt(heads(h, 1, count), q) * (scale * log2e), -1e30)
        e = jnp.exp2(s - jnp.max(s, axis=0, keepdims=True))
        p = e * (use_ref[:, queries] / jnp.sum(e, axis=0, keepdims=True))
        weights = p.astype(BF)
        dprob = nt(heads(h, 2, count), g)
        delta = jnp.sum(p * dprob, axis=0, keepdims=True)
        ds = (p * (dprob - delta) * scale).astype(BF)
        out_t = nn(vt[:, 0:w], weights).astype(BF)
        gq_t = nn(kt[:, 0:w], ds).astype(BF)
        gt[h * HS:(h + 1) * HS, queries] = gq_t
        sq[mine, 0, :, cols] = out_t.T.reshape(BQ // HALF, HALF, HS)
        sq[mine, 1, :, cols] = gq_t.T.reshape(BQ // HALF, HALF, HS)
        gk, gv = nn(ds, q), nn(weights, g)
        if i == SLOTS // BQ - 1:
            gk_acc[...] = gk
            gv_acc[...] = gv
        else:
            gk_acc[0:w] += gk
            gv_acc[0:w] += gv

    def begin_head(h):
        kt[...] = heads(h, 1, CTX).T
        vt[...] = heads(h, 2, CTX).T

    def end_head(h):
        cols = slice(h * HS, (h + 1) * HS)
        for t, acc in ((2, gk_acc), (3, gv_acc)):
            value = acc[...].astype(BF)
            sq[:, t, :, cols] = value.reshape(CTX, HALF, HS)
            gt[(t - 1) * GW + h * HS:(t - 1) * GW + (h + 1) * HS, :] = value.T

    between = {(0, 3): (second, 2), (0, 1): (second, 3), (1, 3): (third, 0), (1, 1): (third, 1)}
    for h in range(2):
        begin_head(h)
        for i in reversed(range(SLOTS // BQ)):
            attend(h, i)
            if (h, i) in between:
                step, k = between[(h, i)]
                step(k)
        end_head(h)

    own_back = pltpu.make_async_copy(sq.at[me], back.at[me], loc_sem.at[0])
    own_back.start()
    out_back = [
        send(sq.at[at(dy, dz)], back.at[me], b_ss.at[i], b_rs.at[i], (dp, at(dy, dz)))
        for i, (dy, dz) in enumerate(OFFSETS)
    ]

    third(2)
    sibling = (xx * 2 + 1 - core, me)
    sums = {}

    def product(k):
        if k >= 2:
            sums["sib", k - 2].wait_send()

        def tile(n, carry):
            part = n // 3
            cols = pl.ds(pl.multiple_of((n % 3) * 256, 256), 256)
            rows = xg[k, part, :, :, :, cols].reshape(SLOTS, 256)
            pb[k % 2, part, :, cols] = nn(gt[...], rows).astype(BF)
            return carry

        lax.fori_loop(0, 6, tile, 0)
        sums["sib", k] = send(
            pb.at[k % 2, 1 - core], sib.at[k], w_ss.at[k], w_rs.at[k], sibling
        )

    def pair(k, lo, hi):
        return pb[k % 2, core, lo:hi].astype(F32) + sib[k, lo:hi].astype(F32)

    def reduce(k):
        sums["sib", k].wait_recv()
        mid = BLOCK // 2
        if k == 0:
            rbuf[0, 0:mid] = pair(k, 0, mid).astype(BF)
            sums["ra"] = send(rbuf.at[0, 0:mid], rel.at[0], w_ss.at[4], w_rs.at[4], (at_x(3), me))
            rbuf[0, mid:] = pair(k, mid, BLOCK).astype(BF)
            sums["rb"] = send(rbuf.at[0, mid:], rel.at[1], w_ss.at[5], w_rs.at[5], (at_x(1), me))
        if k == 1:
            rbuf[1, 0:mid] = pair(k, 0, mid).astype(BF)
            sums["rb"].wait_recv()
            rbuf[1, mid:] = (pair(k, mid, BLOCK) + rel[1].astype(F32)).astype(BF)
            sums["xp"] = send(rbuf.at[1], rx.at[0], w_ss.at[6], w_rs.at[6], (at_x(1), me))
        if k == 2:
            sums["ra"].wait_recv()
            rbuf[2, 0:mid] = (pair(k, 0, mid) + rel[0].astype(F32)).astype(BF)
            rbuf[2, mid:] = pair(k, mid, BLOCK).astype(BF)
            sums["xm"] = send(rbuf.at[2], rx.at[1], w_ss.at[7], w_rs.at[7], (at_x(3), me))
        if k == 3:
            sums["xp"].wait_recv()
            sums["xm"].wait_recv()
            total = pair(k, 0, BLOCK) + rx[0].astype(F32) + rx[1].astype(F32)
            wsum[...] = total * (1.0 / 128.0)

    arrived(0)
    product(0)
    third(3)
    reduce(0)
    for k in range(1, CHUNKS):
        arrived(k)
        product(k)
        reduce(k)

    own_back.wait()
    for copy in out_back:
        copy.wait_recv()
        copy.wait_send()
    for k in range(CHUNKS):
        for copy in stage[k].values():
            copy.wait_send()
    for name in (("sib", 2), ("sib", 3), "ra", "rb", "xp", "xm"):
        sums[name].wait_send()


def finish_kernel(back, wsum, out, gq, gk, gv, weight):
    row = lax.broadcasted_iota(jnp.int32, (ROWS, HALF), 0)
    col = lax.broadcasted_iota(jnp.int32, (ROWS, HALF), 1)
    for group in range(8):
        spread = (row == 2 * col + group % 2).astype(F32).astype(BF)
        for t, ref in enumerate((out, gq, gk, gv)):
            ref[:, group * GW:(group + 1) * GW] = nn(spread, back[group, t]).astype(BF)
    for j in range(3):
        weight[j] = wsum[j * GW:(j + 1) * GW, :].T


def on_device(
    layer_input, query_rows, key_rows, value_rows, out_grad, doc_lengths, dilations, seg_lengths
):
    hbm = pl.BlockSpec(memory_space=pl.ANY)
    smem = pl.BlockSpec(memory_space=pltpu.SMEM)
    vmem = pl.BlockSpec(memory_space=pltpu.VMEM)
    dma = pltpu.SemaphoreType.DMA
    back, wsum = pl.pallas_call(
        kernel,
        out_shape=(
            jax.ShapeDtypeStruct((CTX, 4, HALF, GW), BF),
            jax.ShapeDtypeStruct((BLOCK, BLOCK), F32),
        ),
        in_specs=[hbm] * 5 + [smem] * 3,
        out_specs=(hbm, vmem),
        scratch_shapes=[
            pltpu.VMEM((ROWS, D), BF),
            pltpu.VMEM((4, ROWS, 4096), BF),
            pltpu.VMEM((CTX, 4, HALF, GW), BF),
            pltpu.VMEM((CTX, 4, HALF, GW), BF),
            pltpu.VMEM((CHUNKS, HALF, BLOCK), BF),
            pltpu.VMEM((CHUNKS, 2, SIDE, SIDE, HALF, BLOCK), BF),
            pltpu.VMEM((CHUNKS, 2, SIDE, HALF, BLOCK), BF),
            pltpu.VMEM((3 * GW, SLOTS), BF),
            pltpu.VMEM((SLOTS, 1), jnp.int32),
            pltpu.VMEM((1, SLOTS), jnp.int32),
            pltpu.VMEM((1, SLOTS), F32),
            pltpu.VMEM((HS, SLOTS), BF),
            pltpu.VMEM((HS, SLOTS), BF),
            pltpu.VMEM((SLOTS, HS), F32),
            pltpu.VMEM((SLOTS, HS), F32),
            pltpu.VMEM((2, 2, BLOCK, BLOCK), BF),
            pltpu.VMEM((CHUNKS, BLOCK, BLOCK), BF),
            pltpu.VMEM((3, BLOCK, BLOCK), BF),
            pltpu.VMEM((2, BLOCK // 2, BLOCK), BF),
            pltpu.VMEM((2, BLOCK, BLOCK), BF),
            dma((5,)),
            dma((5,)),
            pltpu.SemaphoreType.REGULAR,
            dma((15,)),
            dma((15,)),
            dma((15,)),
            dma((15,)),
            dma((CHUNKS, 14)),
            dma((CHUNKS, 14)),
            dma((8,)),
            dma((8,)),
        ],
        compiler_params=pltpu.CompilerParams(
            collective_id=0, has_side_effects=True, vmem_limit_bytes=60 * 2**20
        ),
    )(layer_input, query_rows, key_rows, value_rows, out_grad, doc_lengths, dilations, seg_lengths)
    wide = jax.ShapeDtypeStruct((ROWS, 4096), BF)
    out, gq, gk, gv, weight = pl.pallas_call(
        finish_kernel,
        grid=(2,),
        out_shape=(wide, wide, wide, wide, jax.ShapeDtypeStruct((3, BLOCK, GW), F32)),
        in_specs=[
            pl.BlockSpec((8, 4, HALF, GW), lambda i: (i, 0, 0, 0)),
            pl.BlockSpec((BLOCK, BLOCK // 2), lambda i: (0, i)),
        ],
        out_specs=[pl.BlockSpec((ROWS, 2048), lambda i: (0, i))] * 4
        + [pl.BlockSpec((3, BLOCK // 2, GW), lambda i: (0, i, 0))],
        compiler_params=pltpu.CompilerParams(vmem_limit_bytes=40 * 2**20),
    )(back, wsum)
    return out, gq, gk, gv, jnp.transpose(weight, (1, 0, 2))


def solution(mesh):
    rows = P(("dp", "ctx"), None)
    return jax.shard_map(
        on_device,
        mesh=mesh,
        in_specs=(rows, rows, rows, rows, rows, P("dp", None), P(), P()),
        out_specs=(rows, rows, rows, rows, P("dp", None, "ctx")),
        check_vma=False,
    )
```

```python
import functools
import math

import jax
import jax.numpy as jnp
from jax import lax
from jax.experimental import pallas as pl
from jax.experimental.pallas import tpu as pltpu
from jax.sharding import PartitionSpec as P

MESH = pl.DeviceIdType.MESH
HS = 128
SIDE = 4
CTX = 16
ROWS = 128
HALF = 64
SLOTS = 1024
GW = 256
D = 6144
BLOCK = 768
CHUNKS = 4
TILES = 3
UNITS = 6
BQ = 256
BF = jnp.bfloat16
F32 = jnp.float32
SPREAD = (2, 1, 1, 1)


def nt(a, b):
    return lax.dot_general(a, b, (((1,), (1,)), ((), ())), preferred_element_type=F32)


def nn(a, b):
    return jnp.dot(a, b, preferred_element_type=F32)


def slot_ids(shape, dim, parity, group, lengths, rate, seg_len):
    pos = 2 * lax.broadcasted_iota(jnp.int32, shape, dim) + parity
    doc = jnp.zeros(shape, jnp.int32)
    end = jnp.zeros((1, 1), jnp.int32)
    for d in range(16):
        end = end + lengths[:, d:d + 1]
        doc = doc + (pos >= end).astype(jnp.int32)
    seg = jnp.zeros(shape, jnp.int32)
    for m in range(1, 8):
        seg = seg + (pos >= m * seg_len).astype(jnp.int32)
    usable = ((pos - group) & (rate - 1)) == 0
    return doc * 8 + seg, usable


def kernel(
    x_hbm, q_hbm, k_hbm, v_hbm, g_hbm, lengths, rates, segs,
    back, wsum,
    x_in, t_in, len_ref, sq, rq, xs, xg, yb, gt, idk_ref, idq_ref, use_ref, kt, vt, gk_acc, gv_acc,
    r_far, rel, near, rx, fin, ex, ex_in,
    load_sem, loc_sem, l_ss, l_rs, a_ss, a_rs, b_ss, b_rs, x_ss, x_rs, w_ss, w_rs,
):
    dp = lax.axis_index("dp")
    me = lax.axis_index("ctx")
    xx, core = dp // 2, dp % 2
    yy, zz = me // SIDE, me % SIDE
    half, tau = yy // 2, yy % 2
    parity = zz % 2
    group = (half * 2 + core) * SIDE + zz
    at_home = core == tau

    def dev(which, dy, dz):
        return (xx * 2 + which, ((yy + dy) % SIDE) * SIDE + (zz + dz) % SIDE)

    def dev_x(dx):
        return (((xx + dx) % 4) * 2 + core, me)

    sibling = dev(1 - core, 0, 0)

    loads = [
        pltpu.make_async_copy(src, t_in.at[i], load_sem.at[i])
        for i, src in enumerate((q_hbm, k_hbm, v_hbm, g_hbm))
    ]
    loads.append(pltpu.make_async_copy(x_hbm, x_in, load_sem.at[4]))
    for load in loads:
        load.start()
    len_ref[0, 0:1, 0:16] = lengths[...]

    barrier = pltpu.get_barrier_semaphore()
    peers = [
        dev((core + dc) % 2, dy, dz)
        for dc in range(2) for dy in range(SIDE) for dz in range(SIDE) if dc or dy or dz
    ]
    peers += [dev_x(1), dev_x(3)]
    for peer in peers:
        pl.semaphore_signal(barrier, inc=1, device_id=peer, device_id_type=MESH)
    pl.semaphore_wait(barrier, len(peers))

    sent = []

    def send(src, dst, ss, rs, peer):
        copy = pltpu.make_async_remote_copy(
            src_ref=src, dst_ref=dst, send_sem=ss, recv_sem=rs, device_id=peer, device_id_type=MESH
        )
        copy.start()
        sent.append(copy)
        return copy

    def send_or_keep(keep, src, dst, ss, rs, peer):
        copy = pltpu.make_async_remote_copy(
            src_ref=src, dst_ref=dst, send_sem=ss, recv_sem=rs, device_id=peer, device_id_type=MESH
        )

        @pl.when(keep)
        def _():
            pltpu.make_async_copy(src, dst, rs).start()

        @pl.when(jnp.logical_not(keep))
        def _():
            copy.start()

        return copy

    def wait_in(dst, rs):
        pltpu.make_async_copy(dst, dst, rs).wait()

    lens = send(len_ref.at[0], len_ref.at[1], l_ss.at[0], l_rs.at[0], sibling)

    for load in loads[:4]:
        load.wait()
    row = lax.broadcasted_iota(jnp.int32, (HALF, ROWS), 0)
    col = lax.broadcasted_iota(jnp.int32, (HALF, ROWS), 1)
    picks = [(col == 2 * row + par).astype(F32).astype(BF) for par in range(2)]

    def gather_group(two, carry):
        for par in range(2):
            which = 2 * two + par
            cols = pl.ds(pl.multiple_of(which * GW, GW), GW)
            for t in range(4):
                sq[which, t] = nn(picks[par], t_in[t, :, cols]).astype(BF)
        return carry

    lax.fori_loop(0, CTX // 2, gather_group, 0)
    out_q = []
    kept_q = None
    for dz in (0, 1, 3, 2):
        for dh in range(2):
            for kr in range(2):
                there = (half + dh) % 2
                which = (core + kr) % 2
                peer = (xx * 2 + which, (there * 2 + core) * SIDE + (zz + dz) % SIDE)
                src = sq.at[(there * 2 + which) * SIDE + (zz + dz) % SIDE]
                ss = a_ss.at[dh * 8 + dz * 2 + kr]
                rs = a_rs.at[dh * 8 + tau * 4 + dz]
                if dh or dz or kr:
                    out_q.append(send(src, rq.at[me], ss, rs, peer))
                    sent.pop()
                else:
                    kept_q = send_or_keep(at_home, src, rq.at[me], ss, rs, peer)

    loads[4].wait()
    row2 = lax.broadcasted_iota(jnp.int32, (ROWS, ROWS), 0)
    col2 = lax.broadcasted_iota(jnp.int32, (ROWS, ROWS), 1)
    wanted = jnp.where(row2 < HALF, 2 * row2 + parity, 2 * (row2 - HALF) + 1 - parity)
    permute = (col2 == wanted).astype(F32).astype(BF)

    def column(k, which, m):
        if k == 0:
            target, offset = (xx + 2) % 4, m * 128
        elif k == 3:
            target, offset = xx, m * 128
        elif m < 3:
            target, offset = (xx + 1) % 4, (k - 1) * 384 + m * 128
        else:
            target, offset = (xx + 3) % 4, (k - 1) * 384 + (m - 3) * 128
        return pl.ds(pl.multiple_of((target * 2 + which) * BLOCK + offset, 128), 128)

    kept_x = {}

    def first(k):
        z_first = SPREAD[k]
        for which in range(2):
            for n in range(TILES):
                pair = [x_in[:, column(k, which, 2 * n + e)] for e in range(2)]
                both = nn(permute, jnp.concatenate(pair, axis=1)).astype(BF)
                xs[k, which, n, 0] = both[:HALF]
                xs[k, which, n, 1] = both[HALF:]
        slot = jnp.where(at_home, 0, 4)
        for dz in (1, 3, 2, 0):
            for kr in range(2):
                which = (core + kr) % 2
                src = xs.at[k, which, 0:z_first, dz % 2]
                dst = xg.at[k, 0:z_first, slot, zz]
                i = kr * 4 + dz
                if dz or kr:
                    send(src, dst, x_ss.at[k, i], x_rs.at[k, i], dev(which, 0, dz))
                else:
                    pltpu.make_async_copy(src, dst, x_rs.at[k, i]).start()
        shift = jnp.where(at_home, 0, 1)
        for j in range(2):
            for kr in range(2):
                which = (core + kr) % 2
                dy = shift + 2 * j
                src = xs.at[k, which, z_first:TILES]
                dst = yb.at[k, 0:TILES - z_first, :, (SIDE - dy) % SIDE]
                ss, rs = x_ss.at[k, 11 + 2 * j + kr], x_rs.at[k, 11 + dy]
                if j or kr:
                    send(src, dst, ss, rs, dev(which, dy, 0))
                else:
                    kept_x[k] = send_or_keep(at_home, src, dst, ss, rs, dev(which, dy, 0))

    def second(k):
        z_first = SPREAD[k]
        rest = TILES - z_first
        for dy in range(SIDE):
            wait_in(yb.at[k, 0:rest, :, 0], x_rs.at[k, 11 + dy])
        there = xg.at[k, z_first:TILES, 0:SIDE, zz]
        for i, dz in ((15, 1), (16, 3), (17, 2)):
            src = yb.at[k, 0:rest, dz % 2]
            send(src, there, x_ss.at[k, i], x_rs.at[k, i], dev(core, 0, dz))
        pltpu.make_async_copy(yb.at[k, 0:rest, 0], there, loc_sem.at[k]).start()
        for i in range(8):
            wait_in(xg.at[k, 0:z_first, 0, 0], x_rs.at[k, i])
        for i, dy, slot in ((8, 1, 4), (9, 3, 4), (10, 2, 0)):
            src = xg.at[k, 0:z_first, slot]
            dst = xg.at[k, 0:z_first, SIDE - dy]
            send(src, dst, x_ss.at[k, i], x_rs.at[k, i], dev(core, dy, 0))

    def arrived(k):
        z_first = SPREAD[k]
        for i in (8, 9, 10):
            wait_in(xg.at[k, 0:z_first, 0], x_rs.at[k, i])
        there = xg.at[k, z_first:TILES, 0:SIDE, zz]
        wait_in(there, loc_sem.at[k])
        for i in (15, 16, 17):
            wait_in(there, x_rs.at[k, i])

    for k in range(CHUNKS):
        first(k)

    lens.wait_recv()
    own_lengths = jnp.where(at_home, len_ref[0, 0:1, 0:16], len_ref[1, 0:1, 0:16])
    rate, seg_len = rates[group], segs[group]
    ids, usable = slot_ids((SLOTS, 1), 0, parity, group, own_lengths, rate, seg_len)
    idk_ref[...] = jnp.where(usable, ids, -1)
    ids, usable = slot_ids((1, SLOTS), 1, parity, group, own_lengths, rate, seg_len)
    idq_ref[...] = jnp.where(usable, ids, -2)
    use_ref[...] = usable.astype(F32)

    second(0)
    for i in range(CTX):
        wait_in(rq.at[0], a_rs.at[i])
    for copy in out_q:
        copy.wait_send()

    @pl.when(jnp.logical_not(at_home))
    def _():
        kept_q.wait_send()

    scale = 1.0 / math.sqrt(HS)
    log2e = 1.4426950408889634

    def rolled(i):
        return pl.ds(pl.multiple_of(((i + SIDE - yy) % SIDE) * BQ, BQ), BQ)

    def heads(h, t, count):
        return rq[0:count, t, :, h * HS:(h + 1) * HS].reshape(count * HALF, HS)

    def attend(h, i):
        count = (i + 1) * (BQ // HALF)
        w = (i + 1) * BQ
        mine = slice(i * (BQ // HALF), (i + 1) * (BQ // HALF))
        cols = slice(h * HS, (h + 1) * HS)
        q = rq[mine, 0, :, cols].reshape(BQ, HS)
        g = rq[mine, 3, :, cols].reshape(BQ, HS)
        queries = slice(i * BQ, (i + 1) * BQ)
        idq = idq_ref[:, queries]
        allowed = (idk_ref[0:w] == idq) & (
            lax.broadcasted_iota(jnp.int32, (w, BQ), 0)
            <= lax.broadcasted_iota(jnp.int32, (w, BQ), 1) + i * BQ
        )
        s = jnp.where(allowed, nt(heads(h, 1, count), q) * (scale * log2e), -1e30)
        e = jnp.exp2(s - jnp.max(s, axis=0, keepdims=True))
        p = e * (use_ref[:, queries] / jnp.sum(e, axis=0, keepdims=True))
        weights = p.astype(BF)
        dprob = nt(heads(h, 2, count), g)
        delta = jnp.sum(p * dprob, axis=0, keepdims=True)
        ds = (p * (dprob - delta) * scale).astype(BF)
        out_t = nn(vt[:, 0:w], weights).astype(BF)
        gq_t = nn(kt[:, 0:w], ds).astype(BF)
        gt[core, h * HS:(h + 1) * HS, rolled(i)] = gq_t
        sq[mine, 0, :, cols] = out_t.T.reshape(BQ // HALF, HALF, HS)
        sq[mine, 1, :, cols] = gq_t.T.reshape(BQ // HALF, HALF, HS)
        gk, gv = nn(ds, q), nn(weights, g)
        if i == SLOTS // BQ - 1:
            gk_acc[...] = gk
            gv_acc[...] = gv
        else:
            gk_acc[0:w] += gk
            gv_acc[0:w] += gv

    def begin_head(h):
        kt[...] = heads(h, 1, CTX).T
        vt[...] = heads(h, 2, CTX).T

    def end_head(h):
        cols = slice(h * HS, (h + 1) * HS)
        for t, acc in ((2, gk_acc), (3, gv_acc)):
            value = acc[...].astype(BF)
            sq[:, t, :, cols] = value.reshape(CTX, HALF, HS)
            turned = value.T
            rows = slice((t - 1) * GW + h * HS, (t - 1) * GW + (h + 1) * HS)
            for i in range(SLOTS // BQ):
                gt[core, rows, rolled(i)] = turned[:, i * BQ:(i + 1) * BQ]

    between = {(0, 3): 1, (0, 0): 2, (1, 2): 3}
    for h in range(2):
        begin_head(h)
        for i in reversed(range(SLOTS // BQ)):
            attend(h, i)
            if (h, i) in between:
                second(between[(h, i)])
        end_head(h)

    grads = send(gt.at[core], gt.at[core], l_ss.at[1], l_rs.at[1], sibling)
    kept_b = None
    for dy, dz in ((0, 0), (0, 1), (1, 0), (0, 3), (3, 0), (1, 1), (3, 3), (1, 3), (3, 1),
                   (0, 2), (2, 0), (1, 2), (2, 1), (3, 2), (2, 3), (2, 2)):
        peer = dev(tau, dy, dz)
        i = dy // 2 * 8 + dz * 2
        ss, rs = b_ss.at[dy * 4 + dz], b_rs.at[i + core]
        if dy or dz:
            send(sq.at[peer[1]], back.at[group], ss, rs, peer)
        else:
            kept_b = send_or_keep(at_home, sq.at[me], back.at[group], ss, rs, peer)

    def product(k, store):
        def tile(n, carry):
            rows = xg[k, n, 0:SIDE].reshape(SLOTS, 256)
            for g in range(2):
                value = nn(gt[g], rows)
                for e in range(2):
                    store(g, n * 2 + e, value[:, e * 128:(e + 1) * 128])
            return carry

        lax.fori_loop(0, TILES, tile, 0)

    def store_far(g, u, value):
        r_far[g, u] = value.astype(BF)

    def store_near(kk):
        def store(g, u, value):
            near[kk, g, u] = value.astype(BF)
        return store

    def store_own(g, u, value):
        fin[g, u] = value

    grads.wait_recv()
    arrived(0)
    product(0, store_far)
    rel_m = send(r_far.at[0], rel.at[0], w_ss.at[0], w_rs.at[0], dev_x(3))
    rel_p = send(r_far.at[1], rel.at[1], w_ss.at[1], w_rs.at[1], dev_x(1))

    def send_near(kk, g, way):
        i = 2 + kk * 4 + way * 2
        src = near.at[kk, g, way * 3:way * 3 + 3]
        dst = rx.at[way, kk, g]
        send(src, dst, w_ss.at[i + g], w_rs.at[i + g], dev_x(3 if way else 1))

    def relay(kk):
        for u in range(3):
            near[kk, 1, u] = (near[kk, 1, u].astype(F32) + rel[1, kk * 3 + u].astype(F32)).astype(BF)
            near[kk, 0, 3 + u] = (
                near[kk, 0, 3 + u].astype(F32) + rel[0, kk * 3 + u].astype(F32)
            ).astype(BF)

    arrived(1)
    product(1, store_near(0))
    send_near(0, 0, 0)
    send_near(0, 1, 1)
    arrived(2)
    product(2, store_near(1))
    rel_m.wait_recv()
    rel_p.wait_recv()
    relay(0)
    send_near(0, 1, 0)
    send_near(0, 0, 1)
    relay(1)
    send_near(1, 1 - tau, 0)
    send_near(1, 1 - tau, 1)
    send_near(1, tau, 0)
    send_near(1, tau, 1)
    arrived(3)
    product(3, store_own)

    def gathered(kk, g):
        for way in range(2):
            i = 2 + kk * 4 + way * 2
            wait_in(rx.at[way, kk, g], w_rs.at[i + g])

    partner = dev(core, 1 - 2 * tau, 0)
    swaps = []
    for kk in range(2):
        gathered(kk, 1 - tau)
        for u in range(3):
            here = fin[1 - tau, kk * 3 + u] + rx[0, kk, 1 - tau, u].astype(F32)
            ex[kk, u] = (here + rx[1, kk, 1 - tau, u].astype(F32)).astype(BF)
        swaps.append(send(ex.at[kk], ex_in.at[kk], w_ss.at[10 + kk], w_rs.at[10 + kk], partner))
    for kk in range(2):
        gathered(kk, tau)
        for u in range(3):
            here = fin[tau, kk * 3 + u] + rx[0, kk, tau, u].astype(F32)
            fin[tau, kk * 3 + u] = here + rx[1, kk, tau, u].astype(F32)
    for kk in range(2):
        swaps[kk].wait_recv()
        for u in range(3):
            total = fin[tau, kk * 3 + u] + ex_in[kk, u].astype(F32)
            wsum[kk * 3 + u] = total * (1.0 / 128.0)

    for i in range(CTX):
        wait_in(back.at[0], b_rs.at[i])
    for copy in sent:
        copy.wait_send()

    @pl.when(jnp.logical_not(at_home))
    def _():
        kept_b.wait_send()
        for k in range(CHUNKS):
            kept_x[k].wait_send()


def finish_kernel(back, wsum, out, gq, gk, gv, weight):
    row = lax.broadcasted_iota(jnp.int32, (ROWS, HALF), 0)
    col = lax.broadcasted_iota(jnp.int32, (ROWS, HALF), 1)
    for group in range(8):
        spread = (row == 2 * col + group % 2).astype(F32).astype(BF)
        for t, ref in enumerate((out, gq, gk, gv)):
            ref[:, group * GW:(group + 1) * GW] = nn(spread, back[group, t]).astype(BF)
    for u in range(UNITS // 2):
        for j in range(3):
            weight[j, u * 128:(u + 1) * 128] = wsum[u, j * GW:(j + 1) * GW, :].T


def on_device(
    layer_input, query_rows, key_rows, value_rows, out_grad, doc_lengths, dilations, seg_lengths
):
    hbm = pl.BlockSpec(memory_space=pl.ANY)
    smem = pl.BlockSpec(memory_space=pltpu.SMEM)
    vmem = pl.BlockSpec(memory_space=pltpu.VMEM)
    dma = pltpu.SemaphoreType.DMA
    back, wsum = pl.pallas_call(
        kernel,
        out_shape=(
            jax.ShapeDtypeStruct((CTX, 4, HALF, GW), BF),
            jax.ShapeDtypeStruct((UNITS, BLOCK, 128), F32),
        ),
        in_specs=[hbm] * 5 + [vmem] + [smem] * 2,
        out_specs=(hbm, vmem),
        scratch_shapes=[
            pltpu.VMEM((ROWS, D), BF),
            pltpu.VMEM((4, ROWS, 4096), BF),
            pltpu.VMEM((2, 8, 128), jnp.int32),
            pltpu.VMEM((CTX, 4, HALF, GW), BF),
            pltpu.VMEM((CTX, 4, HALF, GW), BF),
            pltpu.VMEM((CHUNKS, 2, TILES, 2, HALF, 256), BF),
            pltpu.VMEM((CHUNKS, TILES, SIDE + 1, SIDE, HALF, 256), BF),
            pltpu.VMEM((CHUNKS, 2, 2, SIDE, HALF, 256), BF),
            pltpu.VMEM((2, 3 * GW, SLOTS), BF),
            pltpu.VMEM((SLOTS, 1), jnp.int32),
            pltpu.VMEM((1, SLOTS), jnp.int32),
            pltpu.VMEM((1, SLOTS), F32),
            pltpu.VMEM((HS, SLOTS), BF),
            pltpu.VMEM((HS, SLOTS), BF),
            pltpu.VMEM((SLOTS, HS), F32),
            pltpu.VMEM((SLOTS, HS), F32),
            pltpu.VMEM((2, UNITS, BLOCK, 128), BF),
            pltpu.VMEM((2, UNITS, BLOCK, 128), BF),
            pltpu.VMEM((2, 2, UNITS, BLOCK, 128), BF),
            pltpu.VMEM((2, 2, 2, 3, BLOCK, 128), BF),
            pltpu.VMEM((2, UNITS, BLOCK, 128), F32),
            pltpu.VMEM((2, 3, BLOCK, 128), BF),
            pltpu.VMEM((2, 3, BLOCK, 128), BF),
            dma((5,)),
            dma((CHUNKS,)),
            dma((2,)),
            dma((2,)),
            dma((CTX,)),
            dma((CTX,)),
            dma((CTX,)),
            dma((CTX,)),
            dma((CHUNKS, 18)),
            dma((CHUNKS, 18)),
            dma((12,)),
            dma((12,)),
        ],
        compiler_params=pltpu.CompilerParams(
            collective_id=0, has_side_effects=True, vmem_limit_bytes=62 * 2**20
        ),
    )(layer_input, query_rows, key_rows, value_rows, out_grad, doc_lengths, dilations, seg_lengths)
    wide = jax.ShapeDtypeStruct((ROWS, 4096), BF)
    out, gq, gk, gv, weight = pl.pallas_call(
        finish_kernel,
        grid=(2,),
        out_shape=(wide, wide, wide, wide, jax.ShapeDtypeStruct((3, BLOCK, GW), F32)),
        in_specs=[
            pl.BlockSpec((8, 4, HALF, GW), lambda i: (i, 0, 0, 0)),
            pl.BlockSpec((UNITS // 2, BLOCK, 128), lambda i: (i, 0, 0)),
        ],
        out_specs=[pl.BlockSpec((ROWS, 2048), lambda i: (0, i))] * 4
        + [pl.BlockSpec((3, BLOCK // 2, GW), lambda i: (0, i, 0))],
        compiler_params=pltpu.CompilerParams(vmem_limit_bytes=62 * 2**20),
    )(back, wsum)
    return out, gq, gk, gv, jnp.transpose(weight, (1, 0, 2))


def solution(mesh):
    rows = P(("dp", "ctx"), None)
    return jax.shard_map(
        on_device,
        mesh=mesh,
        in_specs=(rows, rows, rows, rows, rows, P("dp", None), P(), P()),
        out_specs=(rows, rows, rows, rows, P("dp", None, "ctx")),
        check_vma=False,
    )
```

```python
import functools
import math

import jax
import jax.numpy as jnp
from jax import lax
from jax.experimental import pallas as pl
from jax.experimental.pallas import tpu as pltpu
from jax.sharding import PartitionSpec as P

MESH = pl.DeviceIdType.MESH
HS = 128
SIDE = 4
CTX = 16
ROWS = 128
HALF = 64
SLOTS = 1024
GW = 256
D = 6144
BLOCK = 768
CHUNKS = 4
TILES = 3
UNITS = 6
BQ = 256
BF = jnp.bfloat16
F32 = jnp.float32
SPREAD = (2, 1, 1, 1)


def nt(a, b):
    return lax.dot_general(a, b, (((1,), (1,)), ((), ())), preferred_element_type=F32)


def nn(a, b):
    return jnp.dot(a, b, preferred_element_type=F32)


def slot_ids(shape, dim, parity, group, lengths, rate, seg_len):
    pos = 2 * lax.broadcasted_iota(jnp.int32, shape, dim) + parity
    doc = jnp.zeros(shape, jnp.int32)
    end = jnp.zeros((1, 1), jnp.int32)
    for d in range(16):
        end = end + lengths[:, d:d + 1]
        doc = doc + (pos >= end).astype(jnp.int32)
    seg = jnp.zeros(shape, jnp.int32)
    for m in range(1, 8):
        seg = seg + (pos >= m * seg_len).astype(jnp.int32)
    usable = ((pos - group) & (rate - 1)) == 0
    return doc * 8 + seg, usable


def kernel(
    x_hbm, q_hbm, k_hbm, v_hbm, g_hbm, lengths, rates, segs,
    back, wsum,
    x_in, t_in, len_ref, sq, rq, xs, xg, yb, gt, idk_ref, idq_ref, use_ref, kt, vt, gk_acc, gv_acc,
    r_far, rel, near, rx, fin, ex, ex_in,
    load_sem, loc_sem, l_ss, l_rs, a_ss, a_rs, b_ss, b_rs, x_ss, x_rs, w_ss, w_rs,
):
    dp = lax.axis_index("dp")
    me = lax.axis_index("ctx")
    xx, core = dp // 2, dp % 2
    yy, zz = me // SIDE, me % SIDE
    half, tau = yy // 2, yy % 2
    parity = zz % 2
    group = (half * 2 + core) * SIDE + zz
    at_home = core == tau

    def dev(which, dy, dz):
        return (xx * 2 + which, ((yy + dy) % SIDE) * SIDE + (zz + dz) % SIDE)

    def dev_x(dx):
        return (((xx + dx) % 4) * 2 + core, me)

    sibling = dev(1 - core, 0, 0)

    loads = [
        pltpu.make_async_copy(src, t_in.at[i], load_sem.at[i])
        for i, src in enumerate((q_hbm, k_hbm, v_hbm, g_hbm))
    ]
    loads.append(pltpu.make_async_copy(x_hbm, x_in, load_sem.at[4]))
    for load in loads:
        load.start()
    len_ref[0, 0:1, 0:16] = lengths[...]

    barrier = pltpu.get_barrier_semaphore()
    peers = [
        dev((core + dc) % 2, dy, dz)
        for dc in range(2) for dy in range(SIDE) for dz in range(SIDE) if dc or dy or dz
    ]
    peers += [dev_x(1), dev_x(3)]
    for peer in peers:
        pl.semaphore_signal(barrier, inc=1, device_id=peer, device_id_type=MESH)
    pl.semaphore_wait(barrier, len(peers))

    sent = []

    def send(src, dst, ss, rs, peer):
        copy = pltpu.make_async_remote_copy(
            src_ref=src, dst_ref=dst, send_sem=ss, recv_sem=rs, device_id=peer, device_id_type=MESH
        )
        copy.start()
        sent.append(copy)
        return copy

    def send_or_keep(keep, src, dst, ss, rs, peer):
        copy = pltpu.make_async_remote_copy(
            src_ref=src, dst_ref=dst, send_sem=ss, recv_sem=rs, device_id=peer, device_id_type=MESH
        )

        @pl.when(keep)
        def _():
            pltpu.make_async_copy(src, dst, rs).start()

        @pl.when(jnp.logical_not(keep))
        def _():
            copy.start()

        return copy

    def wait_in(dst, rs):
        pltpu.make_async_copy(dst, dst, rs).wait()

    lens = send(len_ref.at[0], len_ref.at[1], l_ss.at[0], l_rs.at[0], sibling)

    for load in loads[:4]:
        load.wait()
    row = lax.broadcasted_iota(jnp.int32, (HALF, ROWS), 0)
    col = lax.broadcasted_iota(jnp.int32, (HALF, ROWS), 1)
    picks = [(col == 2 * row + par).astype(F32).astype(BF) for par in range(2)]

    def gather_group(two, carry):
        for par in range(2):
            which = 2 * two + par
            cols = pl.ds(pl.multiple_of(which * GW, GW), GW)
            for t in range(4):
                sq[which, t] = nn(picks[par], t_in[t, :, cols]).astype(BF)
        return carry

    lax.fori_loop(0, CTX // 2, gather_group, 0)
    out_q = []
    kept_q = None
    for dz in (0, 1, 3, 2):
        for dh in range(2):
            for kr in range(2):
                there = (half + dh) % 2
                which = (core + kr) % 2
                peer = (xx * 2 + which, (there * 2 + core) * SIDE + (zz + dz) % SIDE)
                src = sq.at[(there * 2 + which) * SIDE + (zz + dz) % SIDE]
                ss = a_ss.at[dh * 8 + dz * 2 + kr]
                rs = a_rs.at[dh * 8 + tau * 4 + dz]
                if dh or dz or kr:
                    out_q.append(send(src, rq.at[me], ss, rs, peer))
                    sent.pop()
                else:
                    kept_q = send_or_keep(at_home, src, rq.at[me], ss, rs, peer)

    loads[4].wait()
    row2 = lax.broadcasted_iota(jnp.int32, (ROWS, ROWS), 0)
    col2 = lax.broadcasted_iota(jnp.int32, (ROWS, ROWS), 1)
    wanted = jnp.where(row2 < HALF, 2 * row2 + parity, 2 * (row2 - HALF) + 1 - parity)
    permute = (col2 == wanted).astype(F32).astype(BF)

    def column(k, which, m):
        if k == 0:
            target, offset = (xx + 2) % 4, m * 128
        elif k == 3:
            target, offset = xx, m * 128
        elif m < 3:
            target, offset = (xx + 1) % 4, (k - 1) * 384 + m * 128
        else:
            target, offset = (xx + 3) % 4, (k - 1) * 384 + (m - 3) * 128
        return pl.ds(pl.multiple_of((target * 2 + which) * BLOCK + offset, 128), 128)

    kept_x = {}

    def prepare(k):
        for which in range(2):
            for n in range(TILES):
                pair = [x_in[:, column(k, which, 2 * n + e)] for e in range(2)]
                both = nn(permute, jnp.concatenate(pair, axis=1)).astype(BF)
                xs[k, which, n, 0] = both[:HALF]
                xs[k, which, n, 1] = both[HALF:]

    def first(k):
        z_first = SPREAD[k]
        slot = jnp.where(at_home, 0, 4)
        for dz in (1, 3, 2, 0):
            for kr in range(2):
                which = (core + kr) % 2
                src = xs.at[k, which, 0:z_first, dz % 2]
                dst = xg.at[k, 0:z_first, slot, zz]
                i = kr * 4 + dz
                if dz or kr:
                    send(src, dst, x_ss.at[k, i], x_rs.at[k, i], dev(which, 0, dz))
                else:
                    pltpu.make_async_copy(src, dst, x_rs.at[k, i]).start()
        shift = jnp.where(at_home, 0, 1)
        for j in range(2):
            for kr in range(2):
                which = (core + kr) % 2
                dy = shift + 2 * j
                src = xs.at[k, which, z_first:TILES]
                dst = yb.at[k, 0:TILES - z_first, :, (SIDE - dy) % SIDE]
                ss, rs = x_ss.at[k, 11 + 2 * j + kr], x_rs.at[k, 11 + dy]
                if j or kr:
                    send(src, dst, ss, rs, dev(which, dy, 0))
                else:
                    kept_x[k] = send_or_keep(at_home, src, dst, ss, rs, dev(which, dy, 0))

    def second(k):
        z_first = SPREAD[k]
        rest = TILES - z_first
        for dy in range(SIDE):
            wait_in(yb.at[k, 0:rest, :, 0], x_rs.at[k, 11 + dy])
        there = xg.at[k, z_first:TILES, 0:SIDE, zz]
        for i, dz in ((15, 1), (16, 3), (17, 2)):
            src = yb.at[k, 0:rest, dz % 2]
            send(src, there, x_ss.at[k, i], x_rs.at[k, i], dev(core, 0, dz))
        pltpu.make_async_copy(yb.at[k, 0:rest, 0], there, loc_sem.at[k]).start()
        for i in range(8):
            wait_in(xg.at[k, 0:z_first, 0, 0], x_rs.at[k, i])
        for i, dy, slot in ((8, 1, 4), (9, 3, 4), (10, 2, 0)):
            src = xg.at[k, 0:z_first, slot]
            dst = xg.at[k, 0:z_first, SIDE - dy]
            send(src, dst, x_ss.at[k, i], x_rs.at[k, i], dev(core, dy, 0))

    def arrived(k):
        z_first = SPREAD[k]
        for i in (8, 9, 10):
            wait_in(xg.at[k, 0:z_first, 0], x_rs.at[k, i])
        there = xg.at[k, z_first:TILES, 0:SIDE, zz]
        wait_in(there, loc_sem.at[k])
        for i in (15, 16, 17):
            wait_in(there, x_rs.at[k, i])

    prepare(0)
    first(0)
    for k in range(1, CHUNKS):
        prepare(k)

    lens.wait_recv()
    own_lengths = jnp.where(at_home, len_ref[0, 0:1, 0:16], len_ref[1, 0:1, 0:16])
    rate, seg_len = rates[group], segs[group]
    ids, usable = slot_ids((SLOTS, 1), 0, parity, group, own_lengths, rate, seg_len)
    idk_ref[...] = jnp.where(usable, ids, -1)
    ids, usable = slot_ids((1, SLOTS), 1, parity, group, own_lengths, rate, seg_len)
    idq_ref[...] = jnp.where(usable, ids, -2)
    use_ref[...] = usable.astype(F32)

    second(0)
    first(1)
    for i in range(CTX):
        wait_in(rq.at[0], a_rs.at[i])
    for copy in out_q:
        copy.wait_send()

    @pl.when(jnp.logical_not(at_home))
    def _():
        kept_q.wait_send()

    scale = 1.0 / math.sqrt(HS)
    log2e = 1.4426950408889634

    def rolled(i):
        return pl.ds(pl.multiple_of(((i + SIDE - yy) % SIDE) * BQ, BQ), BQ)

    def heads(h, t, count):
        return rq[0:count, t, :, h * HS:(h + 1) * HS].reshape(count * HALF, HS)

    def attend(h, i):
        count = (i + 1) * (BQ // HALF)
        w = (i + 1) * BQ
        mine = slice(i * (BQ // HALF), (i + 1) * (BQ // HALF))
        cols = slice(h * HS, (h + 1) * HS)
        q = rq[mine, 0, :, cols].reshape(BQ, HS)
        g = rq[mine, 3, :, cols].reshape(BQ, HS)
        queries = slice(i * BQ, (i + 1) * BQ)
        idq = idq_ref[:, queries]
        allowed = (idk_ref[0:w] == idq) & (
            lax.broadcasted_iota(jnp.int32, (w, BQ), 0)
            <= lax.broadcasted_iota(jnp.int32, (w, BQ), 1) + i * BQ
        )
        s = jnp.where(allowed, nt(heads(h, 1, count), q) * (scale * log2e), -1e30)
        e = jnp.exp2(s - jnp.max(s, axis=0, keepdims=True))
        p = e * (use_ref[:, queries] / jnp.sum(e, axis=0, keepdims=True))
        weights = p.astype(BF)
        dprob = nt(heads(h, 2, count), g)
        delta = jnp.sum(p * dprob, axis=0, keepdims=True)
        ds = (p * (dprob - delta) * scale).astype(BF)
        out_t = nn(vt[:, 0:w], weights).astype(BF)
        gq_t = nn(kt[:, 0:w], ds).astype(BF)
        gt[core, h, 0:HS, rolled(i)] = gq_t
        sq[mine, 0, :, cols] = out_t.T.reshape(BQ // HALF, HALF, HS)
        sq[mine, 1, :, cols] = gq_t.T.reshape(BQ // HALF, HALF, HS)
        gk, gv = nn(ds, q), nn(weights, g)
        if i == SLOTS // BQ - 1:
            gk_acc[...] = gk
            gv_acc[...] = gv
        else:
            gk_acc[0:w] += gk
            gv_acc[0:w] += gv

    def begin_head(h):
        kt[...] = heads(h, 1, CTX).T
        vt[...] = heads(h, 2, CTX).T

    def end_head(h):
        cols = slice(h * HS, (h + 1) * HS)
        for t, acc in ((2, gk_acc), (3, gv_acc)):
            value = acc[...].astype(BF)
            sq[:, t, :, cols] = value.reshape(CTX, HALF, HS)
            turned = value.T
            rows = slice((t - 1) * HS, t * HS)
            for i in range(SLOTS // BQ):
                gt[core, h, rows, rolled(i)] = turned[:, i * BQ:(i + 1) * BQ]

    grads = []
    for h in range(2):
        begin_head(h)
        for i in reversed(range(SLOTS // BQ)):
            attend(h, i)
        end_head(h)
        grads.append(send(gt.at[core, h], gt.at[core, h], l_ss.at[1 + h], l_rs.at[1 + h], sibling))

    def product(k, store):
        def tile(n, carry):
            rows = xg[k, n, 0:SIDE].reshape(SLOTS, 256)
            for g in range(2):
                value = nn(gt[g].reshape(3 * GW, SLOTS), rows)
                for e in range(2):
                    store(g, n * 2 + e, value[:, e * 128:(e + 1) * 128])
            return carry

        lax.fori_loop(0, TILES, tile, 0)

    def store_far(g, u, value):
        r_far[g, u] = value.astype(BF)

    def store_near(kk):
        def store(g, u, value):
            near[kk, g, u] = value.astype(BF)
        return store

    def store_own(g, u, value):
        fin[g, u] = value

    for copy in grads:
        copy.wait_recv()
    arrived(0)
    product(0, store_far)
    rel_m = send(r_far.at[0], rel.at[0], w_ss.at[0], w_rs.at[0], dev_x(3))
    rel_p = send(r_far.at[1], rel.at[1], w_ss.at[1], w_rs.at[1], dev_x(1))

    second(1)
    first(2)
    first(3)

    def send_near(kk, g, way):
        i = 2 + kk * 4 + way * 2
        src = near.at[kk, g, way * 3:way * 3 + 3]
        dst = rx.at[way, kk, g]
        send(src, dst, w_ss.at[i + g], w_rs.at[i + g], dev_x(3 if way else 1))

    def relay(kk):
        for u in range(3):
            near[kk, 1, u] = (near[kk, 1, u].astype(F32) + rel[1, kk * 3 + u].astype(F32)).astype(BF)
            near[kk, 0, 3 + u] = (
                near[kk, 0, 3 + u].astype(F32) + rel[0, kk * 3 + u].astype(F32)
            ).astype(BF)

    arrived(1)
    product(1, store_near(0))
    send_near(0, 0, 0)
    send_near(0, 1, 1)
    second(2)
    second(3)
    rel_m.wait_recv()
    rel_p.wait_recv()
    relay(0)
    send_near(0, 1, 0)
    send_near(0, 0, 1)
    kept_b = None
    for dy, dz in ((0, 0), (0, 1), (1, 0), (0, 3), (3, 0), (1, 1), (3, 3), (1, 3), (3, 1),
                   (0, 2), (2, 0), (1, 2), (2, 1), (3, 2), (2, 3), (2, 2)):
        peer = dev(tau, dy, dz)
        i = dy // 2 * 8 + dz * 2
        ss, rs = b_ss.at[dy * 4 + dz], b_rs.at[i + core]
        if dy or dz:
            send(sq.at[peer[1]], back.at[group], ss, rs, peer)
        else:
            kept_b = send_or_keep(at_home, sq.at[me], back.at[group], ss, rs, peer)

    arrived(2)
    product(2, store_near(1))
    relay(1)
    send_near(1, 1 - tau, 0)
    send_near(1, 1 - tau, 1)
    send_near(1, tau, 0)
    send_near(1, tau, 1)
    arrived(3)
    product(3, store_own)

    def gathered(kk, g):
        for way in range(2):
            i = 2 + kk * 4 + way * 2
            wait_in(rx.at[way, kk, g], w_rs.at[i + g])

    partner = dev(core, 1 - 2 * tau, 0)
    swaps = []
    for kk in range(2):
        gathered(kk, 1 - tau)
        for u in range(3):
            here = fin[1 - tau, kk * 3 + u] + rx[0, kk, 1 - tau, u].astype(F32)
            ex[kk, u] = (here + rx[1, kk, 1 - tau, u].astype(F32)).astype(BF)
        swaps.append(send(ex.at[kk], ex_in.at[kk], w_ss.at[10 + kk], w_rs.at[10 + kk], partner))
    for kk in range(2):
        gathered(kk, tau)
        for u in range(3):
            here = fin[tau, kk * 3 + u] + rx[0, kk, tau, u].astype(F32)
            fin[tau, kk * 3 + u] = here + rx[1, kk, tau, u].astype(F32)
    for kk in range(2):
        swaps[kk].wait_recv()
        for u in range(3):
            total = fin[tau, kk * 3 + u] + ex_in[kk, u].astype(F32)
            wsum[kk * 3 + u] = total * (1.0 / 128.0)

    for i in range(CTX):
        wait_in(back.at[0], b_rs.at[i])
    for copy in sent:
        copy.wait_send()

    @pl.when(jnp.logical_not(at_home))
    def _():
        kept_b.wait_send()
        for k in range(CHUNKS):
            kept_x[k].wait_send()


def finish_kernel(back, wsum, out, gq, gk, gv, weight):
    row = lax.broadcasted_iota(jnp.int32, (ROWS, HALF), 0)
    col = lax.broadcasted_iota(jnp.int32, (ROWS, HALF), 1)
    for group in range(8):
        spread = (row == 2 * col + group % 2).astype(F32).astype(BF)
        for t, ref in enumerate((out, gq, gk, gv)):
            ref[:, group * GW:(group + 1) * GW] = nn(spread, back[group, t]).astype(BF)
    for u in range(UNITS // 2):
        for j in range(3):
            for h in range(2):
                rows = slice((h * 3 + j) * HS, (h * 3 + j + 1) * HS)
                weight[j, u * 128:(u + 1) * 128, h * HS:(h + 1) * HS] = wsum[u, rows, :].T


def on_device(
    layer_input, query_rows, key_rows, value_rows, out_grad, doc_lengths, dilations, seg_lengths
):
    hbm = pl.BlockSpec(memory_space=pl.ANY)
    smem = pl.BlockSpec(memory_space=pltpu.SMEM)
    vmem = pl.BlockSpec(memory_space=pltpu.VMEM)
    dma = pltpu.SemaphoreType.DMA
    back, wsum = pl.pallas_call(
        kernel,
        out_shape=(
            jax.ShapeDtypeStruct((CTX, 4, HALF, GW), BF),
            jax.ShapeDtypeStruct((UNITS, BLOCK, 128), F32),
        ),
        in_specs=[hbm] * 5 + [vmem] + [smem] * 2,
        out_specs=(hbm, vmem),
        scratch_shapes=[
            pltpu.VMEM((ROWS, D), BF),
            pltpu.VMEM((4, ROWS, 4096), BF),
            pltpu.VMEM((2, 8, 128), jnp.int32),
            pltpu.VMEM((CTX, 4, HALF, GW), BF),
            pltpu.VMEM((CTX, 4, HALF, GW), BF),
            pltpu.VMEM((CHUNKS, 2, TILES, 2, HALF, 256), BF),
            pltpu.VMEM((CHUNKS, TILES, SIDE + 1, SIDE, HALF, 256), BF),
            pltpu.VMEM((CHUNKS, 2, 2, SIDE, HALF, 256), BF),
            pltpu.VMEM((2, 2, 3 * HS, SLOTS), BF),
            pltpu.VMEM((SLOTS, 1), jnp.int32),
            pltpu.VMEM((1, SLOTS), jnp.int32),
            pltpu.VMEM((1, SLOTS), F32),
            pltpu.VMEM((HS, SLOTS), BF),
            pltpu.VMEM((HS, SLOTS), BF),
            pltpu.VMEM((SLOTS, HS), F32),
            pltpu.VMEM((SLOTS, HS), F32),
            pltpu.VMEM((2, UNITS, BLOCK, 128), BF),
            pltpu.VMEM((2, UNITS, BLOCK, 128), BF),
            pltpu.VMEM((2, 2, UNITS, BLOCK, 128), BF),
            pltpu.VMEM((2, 2, 2, 3, BLOCK, 128), BF),
            pltpu.VMEM((2, UNITS, BLOCK, 128), F32),
            pltpu.VMEM((2, 3, BLOCK, 128), BF),
            pltpu.VMEM((2, 3, BLOCK, 128), BF),
            dma((5,)),
            dma((CHUNKS,)),
            dma((3,)),
            dma((3,)),
            dma((CTX,)),
            dma((CTX,)),
            dma((CTX,)),
            dma((CTX,)),
            dma((CHUNKS, 18)),
            dma((CHUNKS, 18)),
            dma((12,)),
            dma((12,)),
        ],
        compiler_params=pltpu.CompilerParams(
            collective_id=0, has_side_effects=True, vmem_limit_bytes=62 * 2**20
        ),
    )(layer_input, query_rows, key_rows, value_rows, out_grad, doc_lengths, dilations, seg_lengths)
    wide = jax.ShapeDtypeStruct((ROWS, 4096), BF)
    out, gq, gk, gv, weight = pl.pallas_call(
        finish_kernel,
        grid=(2,),
        out_shape=(wide, wide, wide, wide, jax.ShapeDtypeStruct((3, BLOCK, GW), F32)),
        in_specs=[
            pl.BlockSpec((8, 4, HALF, GW), lambda i: (i, 0, 0, 0)),
            pl.BlockSpec((UNITS // 2, BLOCK, 128), lambda i: (i, 0, 0)),
        ],
        out_specs=[pl.BlockSpec((ROWS, 2048), lambda i: (0, i))] * 4
        + [pl.BlockSpec((3, BLOCK // 2, GW), lambda i: (0, i, 0))],
        compiler_params=pltpu.CompilerParams(vmem_limit_bytes=62 * 2**20),
    )(back, wsum)
    return out, gq, gk, gv, jnp.transpose(weight, (1, 0, 2))


def solution(mesh):
    rows = P(("dp", "ctx"), None)
    return jax.shard_map(
        on_device,
        mesh=mesh,
        in_specs=(rows, rows, rows, rows, rows, P("dp", None), P(), P()),
        out_specs=(rows, rows, rows, rows, P("dp", None, "ctx")),
        check_vma=False,
    )
```

```python
import functools
import math

import jax
import jax.numpy as jnp
from jax import lax
from jax.experimental import pallas as pl
from jax.experimental.pallas import tpu as pltpu
from jax.sharding import PartitionSpec as P

MESH = pl.DeviceIdType.MESH
HS = 128
SIDE = 4
CTX = 16
ROWS = 128
HALF = 64
SLOTS = 1024
GW = 256
D = 6144
BLOCK = 768
CHUNKS = 4
TILES = 3
UNITS = 6
BQ = 256
BF = jnp.bfloat16
F32 = jnp.float32
SPREAD = (2, 1, 1, 1)


def nt(a, b):
    return lax.dot_general(a, b, (((1,), (1,)), ((), ())), preferred_element_type=F32)


def nn(a, b):
    return jnp.dot(a, b, preferred_element_type=F32)


def slot_ids(shape, dim, parity, group, lengths, rate, seg_len):
    pos = 2 * lax.broadcasted_iota(jnp.int32, shape, dim) + parity
    doc = jnp.zeros(shape, jnp.int32)
    end = jnp.zeros((1, 1), jnp.int32)
    for d in range(16):
        end = end + lengths[:, d:d + 1]
        doc = doc + (pos >= end).astype(jnp.int32)
    seg = jnp.zeros(shape, jnp.int32)
    for m in range(1, 8):
        seg = seg + (pos >= m * seg_len).astype(jnp.int32)
    usable = ((pos - group) & (rate - 1)) == 0
    return doc * 8 + seg, usable


def kernel(
    x_hbm, q_hbm, k_hbm, v_hbm, g_hbm, lengths, rates, segs,
    back, wsum,
    x_in, t_in, len_ref, sq, rq, xs, xg, yb, gt, idk_ref, idq_ref, use_ref, kt, vt, gk_acc, gv_acc,
    r_far, rel, near, rx, fin, ex, ex_in,
    load_sem, loc_sem, l_ss, l_rs, a_ss, a_rs, b_ss, b_rs, x_ss, x_rs, w_ss, w_rs,
):
    dp = lax.axis_index("dp")
    me = lax.axis_index("ctx")
    xx, core = dp // 2, dp % 2
    yy, zz = me // SIDE, me % SIDE
    half, tau = yy // 2, yy % 2
    parity = zz % 2
    group = (half * 2 + core) * SIDE + zz
    at_home = core == tau

    def dev(which, dy, dz):
        return (xx * 2 + which, ((yy + dy) % SIDE) * SIDE + (zz + dz) % SIDE)

    def dev_x(dx):
        return (((xx + dx) % 4) * 2 + core, me)

    sibling = dev(1 - core, 0, 0)

    loads = [
        pltpu.make_async_copy(src, t_in.at[i], load_sem.at[i])
        for i, src in enumerate((q_hbm, k_hbm, v_hbm, g_hbm))
    ]
    loads.append(pltpu.make_async_copy(x_hbm, x_in, load_sem.at[4]))
    for load in loads:
        load.start()
    len_ref[0, 0:1, 0:16] = lengths[...]

    barrier = pltpu.get_barrier_semaphore()
    peers = [
        dev((core + dc) % 2, dy, dz)
        for dc in range(2) for dy in range(SIDE) for dz in range(SIDE) if dc or dy or dz
    ]
    peers += [dev_x(1), dev_x(3)]
    for peer in peers:
        pl.semaphore_signal(barrier, inc=1, device_id=peer, device_id_type=MESH)
    pl.semaphore_wait(barrier, len(peers))

    sent = []

    def send(src, dst, ss, rs, peer):
        copy = pltpu.make_async_remote_copy(
            src_ref=src, dst_ref=dst, send_sem=ss, recv_sem=rs, device_id=peer, device_id_type=MESH
        )
        copy.start()
        sent.append(copy)
        return copy

    def send_or_keep(keep, src, dst, ss, rs, peer):
        copy = pltpu.make_async_remote_copy(
            src_ref=src, dst_ref=dst, send_sem=ss, recv_sem=rs, device_id=peer, device_id_type=MESH
        )

        @pl.when(keep)
        def _():
            pltpu.make_async_copy(src, dst, rs).start()

        @pl.when(jnp.logical_not(keep))
        def _():
            copy.start()

        return copy

    def wait_in(dst, rs):
        pltpu.make_async_copy(dst, dst, rs).wait()

    lens = send(len_ref.at[0], len_ref.at[1], l_ss.at[0], l_rs.at[0], sibling)

    for load in loads[:4]:
        load.wait()
    row = lax.broadcasted_iota(jnp.int32, (HALF, ROWS), 0)
    col = lax.broadcasted_iota(jnp.int32, (HALF, ROWS), 1)
    picks = [(col == 2 * row + par).astype(F32).astype(BF) for par in range(2)]

    def gather_group(two, carry):
        for par in range(2):
            which = 2 * two + par
            cols = pl.ds(pl.multiple_of(which * GW, GW), GW)
            for t in range(4):
                sq[which, t] = nn(picks[par], t_in[t, :, cols]).astype(BF)
        return carry

    out_q = []
    kept_q = None
    for dh, order in enumerate((
        ((1, 0), (3, 1), (2, 0), (1, 1), (3, 0), (2, 1), (0, 1), (0, 0)),
        ((0, 1), (1, 0), (3, 1), (0, 0), (1, 1), (3, 0), (2, 0), (2, 1)),
    )):
        base = ((half + dh) % 2) * (CTX // 4)
        lax.fori_loop(base, base + CTX // 4, gather_group, 0)
        for dz, kr in order:
            there = (half + dh) % 2
            which = (core + kr) % 2
            peer = (xx * 2 + which, (there * 2 + core) * SIDE + (zz + dz) % SIDE)
            src = sq.at[(there * 2 + which) * SIDE + (zz + dz) % SIDE]
            ss = a_ss.at[dh * 8 + dz * 2 + kr]
            rs = a_rs.at[dh * 8 + tau * 4 + dz]
            if dh or dz or kr:
                out_q.append(send(src, rq.at[me], ss, rs, peer))
                sent.pop()
            else:
                kept_q = send_or_keep(at_home, src, rq.at[me], ss, rs, peer)

    loads[4].wait()
    row2 = lax.broadcasted_iota(jnp.int32, (ROWS, ROWS), 0)
    col2 = lax.broadcasted_iota(jnp.int32, (ROWS, ROWS), 1)
    wanted = jnp.where(row2 < HALF, 2 * row2 + parity, 2 * (row2 - HALF) + 1 - parity)
    permute = (col2 == wanted).astype(F32).astype(BF)

    def column(k, which, m):
        if k == 0:
            target, offset = (xx + 2) % 4, m * 128
        elif k == 3:
            target, offset = xx, m * 128
        elif m < 3:
            target, offset = (xx + 1) % 4, (k - 1) * 384 + m * 128
        else:
            target, offset = (xx + 3) % 4, (k - 1) * 384 + (m - 3) * 128
        return pl.ds(pl.multiple_of((target * 2 + which) * BLOCK + offset, 128), 128)

    kept_x = {}

    def prepare(k):
        for which in range(2):
            for n in range(TILES):
                pair = [x_in[:, column(k, which, 2 * n + e)] for e in range(2)]
                both = nn(permute, jnp.concatenate(pair, axis=1)).astype(BF)
                xs[k, which, n, 0] = both[:HALF]
                xs[k, which, n, 1] = both[HALF:]

    def first(k):
        z_first = SPREAD[k]
        slot = jnp.where(at_home, 0, 4)
        for dz in (1, 3, 2, 0):
            for kr in range(2):
                which = (core + kr) % 2
                src = xs.at[k, which, 0:z_first, dz % 2]
                dst = xg.at[k, 0:z_first, slot, zz]
                i = kr * 4 + dz
                if dz or kr:
                    send(src, dst, x_ss.at[k, i], x_rs.at[k, i], dev(which, 0, dz))
                else:
                    pltpu.make_async_copy(src, dst, x_rs.at[k, i]).start()
        shift = jnp.where(at_home, 0, 1)
        for j in range(2):
            for kr in range(2):
                which = (core + kr) % 2
                dy = shift + 2 * j
                src = xs.at[k, which, z_first:TILES]
                dst = yb.at[k, 0:TILES - z_first, :, (SIDE - dy) % SIDE]
                ss, rs = x_ss.at[k, 11 + 2 * j + kr], x_rs.at[k, 11 + dy]
                if j or kr:
                    send(src, dst, ss, rs, dev(which, dy, 0))
                else:
                    kept_x[k] = send_or_keep(at_home, src, dst, ss, rs, dev(which, dy, 0))

    def second(k):
        z_first = SPREAD[k]
        rest = TILES - z_first
        for dy in range(SIDE):
            wait_in(yb.at[k, 0:rest, :, 0], x_rs.at[k, 11 + dy])
        there = xg.at[k, z_first:TILES, 0:SIDE, zz]
        for i, dz in ((15, 1), (16, 3), (17, 2)):
            src = yb.at[k, 0:rest, dz % 2]
            send(src, there, x_ss.at[k, i], x_rs.at[k, i], dev(core, 0, dz))
        pltpu.make_async_copy(yb.at[k, 0:rest, 0], there, loc_sem.at[k]).start()
        for i in range(8):
            wait_in(xg.at[k, 0:z_first, 0, 0], x_rs.at[k, i])
        for i, dy, slot in ((8, 1, 4), (9, 3, 4), (10, 2, 0)):
            src = xg.at[k, 0:z_first, slot]
            dst = xg.at[k, 0:z_first, SIDE - dy]
            send(src, dst, x_ss.at[k, i], x_rs.at[k, i], dev(core, dy, 0))

    def arrived(k):
        z_first = SPREAD[k]
        for i in (8, 9, 10):
            wait_in(xg.at[k, 0:z_first, 0], x_rs.at[k, i])
        there = xg.at[k, z_first:TILES, 0:SIDE, zz]
        wait_in(there, loc_sem.at[k])
        for i in (15, 16, 17):
            wait_in(there, x_rs.at[k, i])

    prepare(0)
    first(0)
    for k in range(1, CHUNKS):
        prepare(k)

    lens.wait_recv()
    own_lengths = jnp.where(at_home, len_ref[0, 0:1, 0:16], len_ref[1, 0:1, 0:16])
    rate, seg_len = rates[group], segs[group]
    ids, usable = slot_ids((SLOTS, 1), 0, parity, group, own_lengths, rate, seg_len)
    idk_ref[...] = jnp.where(usable, ids, -1)
    ids, usable = slot_ids((1, SLOTS), 1, parity, group, own_lengths, rate, seg_len)
    idq_ref[...] = jnp.where(usable, ids, -2)
    use_ref[...] = usable.astype(F32)

    second(0)
    first(1)
    first(2)
    first(3)
    for i in range(CTX):
        wait_in(rq.at[0], a_rs.at[i])
    for copy in out_q:
        copy.wait_send()

    @pl.when(jnp.logical_not(at_home))
    def _():
        kept_q.wait_send()

    scale = 1.0 / math.sqrt(HS)
    log2e = 1.4426950408889634

    def rolled(i):
        return pl.ds(pl.multiple_of(((i + SIDE - yy) % SIDE) * BQ, BQ), BQ)

    def heads(h, t, count):
        return rq[0:count, t, :, h * HS:(h + 1) * HS].reshape(count * HALF, HS)

    def attend(h, i):
        count = (i + 1) * (BQ // HALF)
        w = (i + 1) * BQ
        mine = slice(i * (BQ // HALF), (i + 1) * (BQ // HALF))
        cols = slice(h * HS, (h + 1) * HS)
        q = rq[mine, 0, :, cols].reshape(BQ, HS)
        g = rq[mine, 3, :, cols].reshape(BQ, HS)
        queries = slice(i * BQ, (i + 1) * BQ)
        idq = idq_ref[:, queries]
        allowed = (idk_ref[0:w] == idq) & (
            lax.broadcasted_iota(jnp.int32, (w, BQ), 0)
            <= lax.broadcasted_iota(jnp.int32, (w, BQ), 1) + i * BQ
        )
        s = jnp.where(allowed, nt(heads(h, 1, count), q) * (scale * log2e), -1e30)
        e = jnp.exp2(s - jnp.max(s, axis=0, keepdims=True))
        p = e * (use_ref[:, queries] / jnp.sum(e, axis=0, keepdims=True))
        weights = p.astype(BF)
        dprob = nt(heads(h, 2, count), g)
        delta = jnp.sum(p * dprob, axis=0, keepdims=True)
        ds = (p * (dprob - delta) * scale).astype(BF)
        out_t = nn(vt[:, 0:w], weights).astype(BF)
        gq_t = nn(kt[:, 0:w], ds).astype(BF)
        gt[core, h, 0:HS, rolled(i)] = gq_t
        sq[mine, 0, :, cols] = out_t.T.reshape(BQ // HALF, HALF, HS)
        sq[mine, 1, :, cols] = gq_t.T.reshape(BQ // HALF, HALF, HS)
        gk, gv = nn(ds, q), nn(weights, g)
        if i == SLOTS // BQ - 1:
            gk_acc[...] = gk
            gv_acc[...] = gv
        else:
            gk_acc[0:w] += gk
            gv_acc[0:w] += gv

    def begin_head(h):
        kt[...] = heads(h, 1, CTX).T
        vt[...] = heads(h, 2, CTX).T

    def end_head(h):
        cols = slice(h * HS, (h + 1) * HS)
        for t, acc in ((2, gk_acc), (3, gv_acc)):
            value = acc[...].astype(BF)
            sq[:, t, :, cols] = value.reshape(CTX, HALF, HS)
            turned = value.T
            rows = slice((t - 1) * HS, t * HS)
            for i in range(SLOTS // BQ):
                gt[core, h, rows, rolled(i)] = turned[:, i * BQ:(i + 1) * BQ]

    grads = []
    for h in range(2):
        begin_head(h)
        for i in reversed(range(SLOTS // BQ)):
            attend(h, i)
        end_head(h)
        grads.append(send(gt.at[core, h], gt.at[core, h], l_ss.at[1 + h], l_rs.at[1 + h], sibling))

    def product(k, store):
        def tile(n, carry):
            rows = xg[k, n, 0:SIDE].reshape(SLOTS, 256)
            for g in range(2):
                value = nn(gt[g].reshape(3 * GW, SLOTS), rows)
                for e in range(2):
                    store(g, n * 2 + e, value[:, e * 128:(e + 1) * 128])
            return carry

        lax.fori_loop(0, TILES, tile, 0)

    def store_far(g, u, value):
        r_far[g, u] = value.astype(BF)

    def store_near(kk):
        def store(g, u, value):
            near[kk, g, u] = value.astype(BF)
        return store

    def store_own(g, u, value):
        fin[g, u] = value

    for copy in grads:
        copy.wait_recv()
    arrived(0)
    product(0, store_far)
    rel_m = send(r_far.at[0], rel.at[0], w_ss.at[0], w_rs.at[0], dev_x(3))
    rel_p = send(r_far.at[1], rel.at[1], w_ss.at[1], w_rs.at[1], dev_x(1))

    second(1)
    second(2)
    second(3)

    def send_near(kk, g, way):
        i = 2 + kk * 4 + way * 2
        src = near.at[kk, g, pl.ds(way * 3, 3)]
        dst = rx.at[way, kk, g]
        send(src, dst, w_ss.at[i + g], w_rs.at[i + g], dev_x(1 + 2 * way))

    def relay(kk):
        for u in range(3):
            near[kk, 1, u] = (near[kk, 1, u].astype(F32) + rel[1, kk * 3 + u].astype(F32)).astype(BF)
            near[kk, 0, 3 + u] = (
                near[kk, 0, 3 + u].astype(F32) + rel[0, kk * 3 + u].astype(F32)
            ).astype(BF)

    other = 1 - tau
    arrived(1)
    product(1, store_near(0))
    send_near(0, other, other)
    rel_m.wait_recv()
    rel_p.wait_recv()
    relay(0)
    send_near(0, other, tau)
    kept_b = None
    for dy, dz in ((0, 0), (0, 1), (1, 0), (0, 3), (3, 0), (1, 1), (3, 3), (1, 3), (3, 1),
                   (0, 2), (2, 0), (1, 2), (2, 1), (3, 2), (2, 3), (2, 2)):
        peer = dev(tau, dy, dz)
        i = dy // 2 * 8 + dz * 2
        ss, rs = b_ss.at[dy * 4 + dz], b_rs.at[i + core]
        if dy or dz:
            send(sq.at[peer[1]], back.at[group], ss, rs, peer)
        else:
            kept_b = send_or_keep(at_home, sq.at[me], back.at[group], ss, rs, peer)

    arrived(2)
    product(2, store_near(1))
    relay(1)
    for kk, g in ((1, other), (0, tau), (1, tau)):
        for way in range(2):
            send_near(kk, g, way)
    arrived(3)
    product(3, store_own)

    def gathered(kk, g):
        for way in range(2):
            i = 2 + kk * 4 + way * 2
            wait_in(rx.at[way, kk, g], w_rs.at[i + g])

    partner = dev(core, 1 - 2 * tau, 0)
    swaps = []
    for kk in range(2):
        gathered(kk, 1 - tau)
        for u in range(3):
            here = fin[1 - tau, kk * 3 + u] + rx[0, kk, 1 - tau, u].astype(F32)
            ex[kk, u] = (here + rx[1, kk, 1 - tau, u].astype(F32)).astype(BF)
        swaps.append(send(ex.at[kk], ex_in.at[kk], w_ss.at[10 + kk], w_rs.at[10 + kk], partner))
    for kk in range(2):
        gathered(kk, tau)
        for u in range(3):
            here = fin[tau, kk * 3 + u] + rx[0, kk, tau, u].astype(F32)
            fin[tau, kk * 3 + u] = here + rx[1, kk, tau, u].astype(F32)
    for kk in range(2):
        swaps[kk].wait_recv()
        for u in range(3):
            total = fin[tau, kk * 3 + u] + ex_in[kk, u].astype(F32)
            wsum[kk * 3 + u] = total * (1.0 / 128.0)

    for i in range(CTX):
        wait_in(back.at[0], b_rs.at[i])
    for copy in sent:
        copy.wait_send()

    @pl.when(jnp.logical_not(at_home))
    def _():
        kept_b.wait_send()
        for k in range(CHUNKS):
            kept_x[k].wait_send()


def finish_kernel(back, wsum, out, gq, gk, gv, weight):
    row = lax.broadcasted_iota(jnp.int32, (ROWS, HALF), 0)
    col = lax.broadcasted_iota(jnp.int32, (ROWS, HALF), 1)
    for group in range(8):
        spread = (row == 2 * col + group % 2).astype(F32).astype(BF)
        for t, ref in enumerate((out, gq, gk, gv)):
            ref[:, group * GW:(group + 1) * GW] = nn(spread, back[group, t]).astype(BF)
    for u in range(UNITS // 2):
        for j in range(3):
            for h in range(2):
                rows = slice((h * 3 + j) * HS, (h * 3 + j + 1) * HS)
                weight[j, u * 128:(u + 1) * 128, h * HS:(h + 1) * HS] = wsum[u, rows, :].T


def on_device(
    layer_input, query_rows, key_rows, value_rows, out_grad, doc_lengths, dilations, seg_lengths
):
    hbm = pl.BlockSpec(memory_space=pl.ANY)
    smem = pl.BlockSpec(memory_space=pltpu.SMEM)
    vmem = pl.BlockSpec(memory_space=pltpu.VMEM)
    dma = pltpu.SemaphoreType.DMA
    back, wsum = pl.pallas_call(
        kernel,
        out_shape=(
            jax.ShapeDtypeStruct((CTX, 4, HALF, GW), BF),
            jax.ShapeDtypeStruct((UNITS, BLOCK, 128), F32),
        ),
        in_specs=[hbm] * 5 + [vmem] + [smem] * 2,
        out_specs=(hbm, vmem),
        scratch_shapes=[
            pltpu.VMEM((ROWS, D), BF),
            pltpu.VMEM((4, ROWS, 4096), BF),
            pltpu.VMEM((2, 8, 128), jnp.int32),
            pltpu.VMEM((CTX, 4, HALF, GW), BF),
            pltpu.VMEM((CTX, 4, HALF, GW), BF),
            pltpu.VMEM((CHUNKS, 2, TILES, 2, HALF, 256), BF),
            pltpu.VMEM((CHUNKS, TILES, SIDE + 1, SIDE, HALF, 256), BF),
            pltpu.VMEM((CHUNKS, 2, 2, SIDE, HALF, 256), BF),
            pltpu.VMEM((2, 2, 3 * HS, SLOTS), BF),
            pltpu.VMEM((SLOTS, 1), jnp.int32),
            pltpu.VMEM((1, SLOTS), jnp.int32),
            pltpu.VMEM((1, SLOTS), F32),
            pltpu.VMEM((HS, SLOTS), BF),
            pltpu.VMEM((HS, SLOTS), BF),
            pltpu.VMEM((SLOTS, HS), F32),
            pltpu.VMEM((SLOTS, HS), F32),
            pltpu.VMEM((2, UNITS, BLOCK, 128), BF),
            pltpu.VMEM((2, UNITS, BLOCK, 128), BF),
            pltpu.VMEM((2, 2, UNITS, BLOCK, 128), BF),
            pltpu.VMEM((2, 2, 2, 3, BLOCK, 128), BF),
            pltpu.VMEM((2, UNITS, BLOCK, 128), F32),
            pltpu.VMEM((2, 3, BLOCK, 128), BF),
            pltpu.VMEM((2, 3, BLOCK, 128), BF),
            dma((5,)),
            dma((CHUNKS,)),
            dma((3,)),
            dma((3,)),
            dma((CTX,)),
            dma((CTX,)),
            dma((CTX,)),
            dma((CTX,)),
            dma((CHUNKS, 18)),
            dma((CHUNKS, 18)),
            dma((12,)),
            dma((12,)),
        ],
        compiler_params=pltpu.CompilerParams(
            collective_id=0, has_side_effects=True, vmem_limit_bytes=62 * 2**20
        ),
    )(layer_input, query_rows, key_rows, value_rows, out_grad, doc_lengths, dilations, seg_lengths)
    wide = jax.ShapeDtypeStruct((ROWS, 4096), BF)
    out, gq, gk, gv, weight = pl.pallas_call(
        finish_kernel,
        grid=(2,),
        out_shape=(wide, wide, wide, wide, jax.ShapeDtypeStruct((3, BLOCK, GW), F32)),
        in_specs=[
            pl.BlockSpec((8, 4, HALF, GW), lambda i: (i, 0, 0, 0)),
            pl.BlockSpec((UNITS // 2, BLOCK, 128), lambda i: (i, 0, 0)),
        ],
        out_specs=[pl.BlockSpec((ROWS, 2048), lambda i: (0, i))] * 4
        + [pl.BlockSpec((3, BLOCK // 2, GW), lambda i: (0, i, 0))],
        compiler_params=pltpu.CompilerParams(vmem_limit_bytes=62 * 2**20),
    )(back, wsum)
    return out, gq, gk, gv, jnp.transpose(weight, (1, 0, 2))


def solution(mesh):
    rows = P(("dp", "ctx"), None)
    return jax.shard_map(
        on_device,
        mesh=mesh,
        in_specs=(rows, rows, rows, rows, rows, P("dp", None), P(), P()),
        out_specs=(rows, rows, rows, rows, P("dp", None, "ctx")),
        check_vma=False,
    )
```

```python
import functools
import math

import jax
import jax.numpy as jnp
from jax import lax
from jax.experimental import pallas as pl
from jax.experimental.pallas import tpu as pltpu
from jax.sharding import PartitionSpec as P

MESH = pl.DeviceIdType.MESH
HS = 128
SIDE = 4
CTX = 16
ROWS = 128
HALF = 64
SLOTS = 1024
GW = 256
D = 6144
BLOCK = 768
CHUNKS = 4
TILES = 3
UNITS = 6
BQ = 256
BF = jnp.bfloat16
F32 = jnp.float32
SPREAD = (2, 1, 1, 1)


def nt(a, b):
    return lax.dot_general(a, b, (((1,), (1,)), ((), ())), preferred_element_type=F32)


def nn(a, b):
    return jnp.dot(a, b, preferred_element_type=F32)


def slot_ids(shape, dim, parity, group, lengths, rate, seg_len):
    pos = 2 * lax.broadcasted_iota(jnp.int32, shape, dim) + parity
    doc = jnp.zeros(shape, jnp.int32)
    end = jnp.zeros((1, 1), jnp.int32)
    for d in range(16):
        end = end + lengths[:, d:d + 1]
        doc = doc + (pos >= end).astype(jnp.int32)
    seg = jnp.zeros(shape, jnp.int32)
    for m in range(1, 8):
        seg = seg + (pos >= m * seg_len).astype(jnp.int32)
    usable = ((pos - group) & (rate - 1)) == 0
    return doc * 8 + seg, usable


def kernel(
    x_hbm, q_hbm, k_hbm, v_hbm, g_hbm, lengths, rates, segs,
    back, wsum,
    x_in, t_in, len_ref, sq, rq, xs, xg, yb, gt, idk_ref, idq_ref, use_ref, kt, vt, gk_acc, gv_acc,
    r_far, rel, near, rx, fin, ex, ex_in,
    load_sem, loc_sem, l_ss, l_rs, a_ss, a_rs, b_ss, b_rs, x_ss, x_rs, w_ss, w_rs,
):
    dp = lax.axis_index("dp")
    me = lax.axis_index("ctx")
    xx, core = dp // 2, dp % 2
    yy, zz = me // SIDE, me % SIDE
    half, tau = yy // 2, yy % 2
    parity = zz % 2
    group = (half * 2 + core) * SIDE + zz
    at_home = core == tau

    def dev(which, dy, dz):
        return (xx * 2 + which, ((yy + dy) % SIDE) * SIDE + (zz + dz) % SIDE)

    def dev_x(dx):
        return (((xx + dx) % 4) * 2 + core, me)

    sibling = dev(1 - core, 0, 0)

    loads = [
        pltpu.make_async_copy(src, t_in.at[i], load_sem.at[i])
        for i, src in enumerate((q_hbm, k_hbm, v_hbm, g_hbm))
    ]
    loads.append(pltpu.make_async_copy(x_hbm, x_in, load_sem.at[4]))
    for load in loads:
        load.start()
    len_ref[0, 0:1, 0:16] = lengths[...]

    barrier = pltpu.get_barrier_semaphore()
    peers = [
        dev((core + dc) % 2, dy, dz)
        for dc in range(2) for dy in range(SIDE) for dz in range(SIDE) if dc or dy or dz
    ]
    peers += [dev_x(1), dev_x(3)]
    for peer in peers:
        pl.semaphore_signal(barrier, inc=1, device_id=peer, device_id_type=MESH)
    pl.semaphore_wait(barrier, len(peers))

    sent = []

    def send(src, dst, ss, rs, peer):
        copy = pltpu.make_async_remote_copy(
            src_ref=src, dst_ref=dst, send_sem=ss, recv_sem=rs, device_id=peer, device_id_type=MESH
        )
        copy.start()
        sent.append(copy)
        return copy

    def send_or_keep(keep, src, dst, ss, rs, peer):
        copy = pltpu.make_async_remote_copy(
            src_ref=src, dst_ref=dst, send_sem=ss, recv_sem=rs, device_id=peer, device_id_type=MESH
        )

        @pl.when(keep)
        def _():
            pltpu.make_async_copy(src, dst, rs).start()

        @pl.when(jnp.logical_not(keep))
        def _():
            copy.start()

        return copy

    def wait_in(dst, rs):
        pltpu.make_async_copy(dst, dst, rs).wait()

    lens = send(len_ref.at[0], len_ref.at[1], l_ss.at[0], l_rs.at[0], sibling)

    for load in loads[:4]:
        load.wait()
    row = lax.broadcasted_iota(jnp.int32, (HALF, ROWS), 0)
    col = lax.broadcasted_iota(jnp.int32, (HALF, ROWS), 1)
    picks = [(col == 2 * row + par).astype(F32).astype(BF) for par in range(2)]

    def gather_group(two, carry):
        for par in range(2):
            which = 2 * two + par
            cols = pl.ds(pl.multiple_of(which * GW, GW), GW)
            for t in range(4):
                sq[which, t] = nn(picks[par], t_in[t, :, cols]).astype(BF)
        return carry

    out_q = []
    kept_q = None
    for dh, order in enumerate((
        ((1, 0), (3, 1), (2, 0), (1, 1), (3, 0), (2, 1), (0, 1), (0, 0)),
        ((0, 1), (1, 0), (3, 1), (0, 0), (1, 1), (3, 0), (2, 0), (2, 1)),
    )):
        base = ((half + dh) % 2) * (CTX // 4)
        lax.fori_loop(base, base + CTX // 4, gather_group, 0)
        for dz, kr in order:
            there = (half + dh) % 2
            which = (core + kr) % 2
            peer = (xx * 2 + which, (there * 2 + core) * SIDE + (zz + dz) % SIDE)
            src = sq.at[(there * 2 + which) * SIDE + (zz + dz) % SIDE]
            ss = a_ss.at[dh * 8 + dz * 2 + kr]
            rs = a_rs.at[dh * 8 + tau * 4 + dz]
            if dh or dz or kr:
                out_q.append(send(src, rq.at[me], ss, rs, peer))
                sent.pop()
            else:
                kept_q = send_or_keep(at_home, src, rq.at[me], ss, rs, peer)

    loads[4].wait()
    row2 = lax.broadcasted_iota(jnp.int32, (ROWS, ROWS), 0)
    col2 = lax.broadcasted_iota(jnp.int32, (ROWS, ROWS), 1)
    wanted = jnp.where(row2 < HALF, 2 * row2 + parity, 2 * (row2 - HALF) + 1 - parity)
    permute = (col2 == wanted).astype(F32).astype(BF)

    def column(k, which, m):
        if k == 0:
            target, offset = (xx + 2) % 4, m * 128
        elif k == 3:
            target, offset = xx, m * 128
        elif m < 3:
            target, offset = (xx + 1) % 4, (k - 1) * 384 + m * 128
        else:
            target, offset = (xx + 3) % 4, (k - 1) * 384 + (m - 3) * 128
        return pl.ds(pl.multiple_of((target * 2 + which) * BLOCK + offset, 128), 128)

    kept_x = {}

    def prepare(k):
        for which in range(2):
            for n in range(TILES):
                pair = [x_in[:, column(k, which, 2 * n + e)] for e in range(2)]
                both = nn(permute, jnp.concatenate(pair, axis=1)).astype(BF)
                xs[k, which, n, 0] = both[:HALF]
                xs[k, which, n, 1] = both[HALF:]

    def first(k):
        z_first = SPREAD[k]
        slot = jnp.where(at_home, 0, 4)
        for dz in (1, 3, 2, 0):
            for kr in range(2):
                which = (core + kr) % 2
                src = xs.at[k, which, 0:z_first, dz % 2]
                dst = xg.at[k, 0:z_first, slot, zz]
                i = kr * 4 + dz
                if dz or kr:
                    send(src, dst, x_ss.at[k, i], x_rs.at[k, i], dev(which, 0, dz))
                else:
                    pltpu.make_async_copy(src, dst, x_rs.at[k, i]).start()
        shift = jnp.where(at_home, 0, 1)
        for j in range(2):
            for kr in range(2):
                which = (core + kr) % 2
                dy = shift + 2 * j
                src = xs.at[k, which, z_first:TILES]
                dst = yb.at[k, 0:TILES - z_first, :, (SIDE - dy) % SIDE]
                ss, rs = x_ss.at[k, 11 + 2 * j + kr], x_rs.at[k, 11 + dy]
                if j or kr:
                    send(src, dst, ss, rs, dev(which, dy, 0))
                else:
                    kept_x[k] = send_or_keep(at_home, src, dst, ss, rs, dev(which, dy, 0))

    def second(k):
        z_first = SPREAD[k]
        rest = TILES - z_first
        for dy in range(SIDE):
            wait_in(yb.at[k, 0:rest, :, 0], x_rs.at[k, 11 + dy])
        there = xg.at[k, z_first:TILES, 0:SIDE, zz]
        for i, dz in ((15, 1), (16, 3), (17, 2)):
            src = yb.at[k, 0:rest, dz % 2]
            send(src, there, x_ss.at[k, i], x_rs.at[k, i], dev(core, 0, dz))
        pltpu.make_async_copy(yb.at[k, 0:rest, 0], there, loc_sem.at[k]).start()
        for i in range(8):
            wait_in(xg.at[k, 0:z_first, 0, 0], x_rs.at[k, i])
        for i, dy, slot in ((8, 1, 4), (9, 3, 4), (10, 2, 0)):
            src = xg.at[k, 0:z_first, slot]
            dst = xg.at[k, 0:z_first, SIDE - dy]
            send(src, dst, x_ss.at[k, i], x_rs.at[k, i], dev(core, dy, 0))

    def arrived(k):
        z_first = SPREAD[k]
        for i in (8, 9, 10):
            wait_in(xg.at[k, 0:z_first, 0], x_rs.at[k, i])
        there = xg.at[k, z_first:TILES, 0:SIDE, zz]
        wait_in(there, loc_sem.at[k])
        for i in (15, 16, 17):
            wait_in(there, x_rs.at[k, i])

    prepare(0)
    first(0)
    for k in range(1, CHUNKS):
        prepare(k)

    lens.wait_recv()
    own_lengths = jnp.where(at_home, len_ref[0, 0:1, 0:16], len_ref[1, 0:1, 0:16])
    rate, seg_len = rates[group], segs[group]
    ids, usable = slot_ids((SLOTS, 1), 0, parity, group, own_lengths, rate, seg_len)
    idk_ref[...] = jnp.where(usable, ids, -1)
    ids, usable = slot_ids((1, SLOTS), 1, parity, group, own_lengths, rate, seg_len)
    idq_ref[...] = jnp.where(usable, ids, -2)
    use_ref[...] = usable.astype(F32)

    second(0)
    first(1)
    first(2)
    first(3)
    for i in range(CTX):
        wait_in(rq.at[0], a_rs.at[i])
    for copy in out_q:
        copy.wait_send()

    @pl.when(jnp.logical_not(at_home))
    def _():
        kept_q.wait_send()

    scale = 1.0 / math.sqrt(HS)
    log2e = 1.4426950408889634

    def rolled(i):
        return pl.ds(pl.multiple_of(((i + SIDE - yy) % SIDE) * BQ, BQ), BQ)

    def heads(h, t, count):
        return rq[0:count, t, :, h * HS:(h + 1) * HS].reshape(count * HALF, HS)

    def attend(h, i):
        count = (i + 1) * (BQ // HALF)
        w = (i + 1) * BQ
        mine = slice(i * (BQ // HALF), (i + 1) * (BQ // HALF))
        cols = slice(h * HS, (h + 1) * HS)
        q = rq[mine, 0, :, cols].reshape(BQ, HS)
        g = rq[mine, 3, :, cols].reshape(BQ, HS)
        queries = slice(i * BQ, (i + 1) * BQ)
        idq = idq_ref[:, queries]
        allowed = (idk_ref[0:w] == idq) & (
            lax.broadcasted_iota(jnp.int32, (w, BQ), 0)
            <= lax.broadcasted_iota(jnp.int32, (w, BQ), 1) + i * BQ
        )
        s = jnp.where(allowed, nt(heads(h, 1, count), q) * (scale * log2e), -1e30)
        e = jnp.exp2(s - jnp.max(s, axis=0, keepdims=True))
        p = e * (use_ref[:, queries] / jnp.sum(e, axis=0, keepdims=True))
        weights = p.astype(BF)
        dprob = nt(heads(h, 2, count), g)
        delta = jnp.sum(p * dprob, axis=0, keepdims=True)
        ds = (p * (dprob - delta) * scale).astype(BF)
        out_t = nn(vt[:, 0:w], weights).astype(BF)
        gq_t = nn(kt[:, 0:w], ds).astype(BF)
        gt[core, h, 0:HS, rolled(i)] = gq_t
        sq[mine, 0, :, cols] = out_t.T.reshape(BQ // HALF, HALF, HS)
        sq[mine, 1, :, cols] = gq_t.T.reshape(BQ // HALF, HALF, HS)
        gk, gv = nn(ds, q), nn(weights, g)
        if i == SLOTS // BQ - 1:
            gk_acc[...] = gk
            gv_acc[...] = gv
        else:
            gk_acc[0:w] += gk
            gv_acc[0:w] += gv

    def begin_head(h):
        kt[...] = heads(h, 1, CTX).T
        vt[...] = heads(h, 2, CTX).T

    def end_head(h):
        cols = slice(h * HS, (h + 1) * HS)
        for t, acc in ((2, gk_acc), (3, gv_acc)):
            value = acc[...].astype(BF)
            sq[:, t, :, cols] = value.reshape(CTX, HALF, HS)
            turned = value.T
            rows = slice((t - 1) * HS, t * HS)
            for i in range(SLOTS // BQ):
                gt[core, h, rows, rolled(i)] = turned[:, i * BQ:(i + 1) * BQ]

    grads = []
    for h in range(2):
        begin_head(h)
        for i in reversed(range(SLOTS // BQ)):
            attend(h, i)
        end_head(h)
        grads.append(send(gt.at[core, h], gt.at[core, h], l_ss.at[1 + h], l_rs.at[1 + h], sibling))

    def product(k, store, groups=(0, 1)):
        def tile(n, carry):
            rows = xg[k, n, 0:SIDE].reshape(SLOTS, 256)
            for g in groups:
                value = nn(gt[g].reshape(3 * GW, SLOTS), rows)
                for e in range(2):
                    store(g, n * 2 + e, value[:, e * 128:(e + 1) * 128])
            return carry

        lax.fori_loop(0, TILES, tile, 0)

    def store_far(g, u, value):
        r_far[g, u] = value.astype(BF)

    def store_near(kk):
        def store(g, u, value):
            near[kk, g, u] = value.astype(BF)
        return store

    def store_own(g, u, value):
        fin[g, u] = value

    arrived(0)
    rels = []
    for g in (core, 1 - core):
        if rels:
            for copy in grads:
                copy.wait_recv()
        product(0, store_far, (g,))
        to = dev_x(jnp.where(g == 0, 3, 1))
        rels.append(send(r_far.at[g], rel.at[g], w_ss.at[g], w_rs.at[g], to))

    second(1)
    second(2)
    second(3)

    def send_near(kk, g, way):
        i = 2 + kk * 4 + way * 2
        src = near.at[kk, g, pl.ds(way * 3, 3)]
        dst = rx.at[way, kk, g]
        send(src, dst, w_ss.at[i + g], w_rs.at[i + g], dev_x(1 + 2 * way))

    def relay(kk):
        for u in range(3):
            near[kk, 1, u] = (near[kk, 1, u].astype(F32) + rel[1, kk * 3 + u].astype(F32)).astype(BF)
            near[kk, 0, 3 + u] = (
                near[kk, 0, 3 + u].astype(F32) + rel[0, kk * 3 + u].astype(F32)
            ).astype(BF)

    other = 1 - tau
    arrived(1)
    product(1, store_near(0))
    send_near(0, other, other)
    kept_b = None
    for dy, dz in ((0, 0), (0, 1), (1, 0), (0, 3), (3, 0), (1, 1), (3, 3), (1, 3), (3, 1),
                   (0, 2), (2, 0), (1, 2), (2, 1), (3, 2), (2, 3), (2, 2)):
        peer = dev(tau, dy, dz)
        i = dy // 2 * 8 + dz * 2
        ss, rs = b_ss.at[dy * 4 + dz], b_rs.at[i + core]
        if dy or dz:
            send(sq.at[peer[1]], back.at[group], ss, rs, peer)
        else:
            kept_b = send_or_keep(at_home, sq.at[me], back.at[group], ss, rs, peer)

    for copy in rels:
        copy.wait_recv()
    relay(0)
    send_near(0, other, tau)
    arrived(2)
    product(2, store_near(1))
    relay(1)
    for kk, g in ((1, other), (0, tau), (1, tau)):
        for way in range(2):
            send_near(kk, g, way)
    arrived(3)
    product(3, store_own)

    def gathered(kk, g):
        for way in range(2):
            i = 2 + kk * 4 + way * 2
            wait_in(rx.at[way, kk, g], w_rs.at[i + g])

    partner = dev(core, 1 - 2 * tau, 0)
    swaps = []
    for kk in range(2):
        gathered(kk, 1 - tau)
        for u in range(3):
            here = fin[1 - tau, kk * 3 + u] + rx[0, kk, 1 - tau, u].astype(F32)
            ex[kk, u] = (here + rx[1, kk, 1 - tau, u].astype(F32)).astype(BF)
        swaps.append(send(ex.at[kk], ex_in.at[kk], w_ss.at[10 + kk], w_rs.at[10 + kk], partner))
    for kk in range(2):
        gathered(kk, tau)
        swaps[kk].wait_recv()
        for u in range(3):
            here = fin[tau, kk * 3 + u] + rx[0, kk, tau, u].astype(F32)
            here = here + rx[1, kk, tau, u].astype(F32) + ex_in[kk, u].astype(F32)
            wsum[kk * 3 + u] = here * (1.0 / 128.0)

    for i in range(CTX):
        wait_in(back.at[0], b_rs.at[i])
    for copy in sent:
        copy.wait_send()

    @pl.when(jnp.logical_not(at_home))
    def _():
        kept_b.wait_send()
        for k in range(CHUNKS):
            kept_x[k].wait_send()


def finish_kernel(back, wsum, out, gq, gk, gv, weight):
    row = lax.broadcasted_iota(jnp.int32, (ROWS, HALF), 0)
    col = lax.broadcasted_iota(jnp.int32, (ROWS, HALF), 1)
    for group in range(8):
        spread = (row == 2 * col + group % 2).astype(F32).astype(BF)
        for t, ref in enumerate((out, gq, gk, gv)):
            ref[:, group * GW:(group + 1) * GW] = nn(spread, back[group, t]).astype(BF)
    for u in range(UNITS // 2):
        for j in range(3):
            for h in range(2):
                rows = slice((h * 3 + j) * HS, (h * 3 + j + 1) * HS)
                weight[j, u * 128:(u + 1) * 128, h * HS:(h + 1) * HS] = wsum[u, rows, :].T


def on_device(
    layer_input, query_rows, key_rows, value_rows, out_grad, doc_lengths, dilations, seg_lengths
):
    hbm = pl.BlockSpec(memory_space=pl.ANY)
    smem = pl.BlockSpec(memory_space=pltpu.SMEM)
    vmem = pl.BlockSpec(memory_space=pltpu.VMEM)
    dma = pltpu.SemaphoreType.DMA
    back, wsum = pl.pallas_call(
        kernel,
        out_shape=(
            jax.ShapeDtypeStruct((CTX, 4, HALF, GW), BF),
            jax.ShapeDtypeStruct((UNITS, BLOCK, 128), F32),
        ),
        in_specs=[hbm] * 5 + [vmem] + [smem] * 2,
        out_specs=(hbm, vmem),
        scratch_shapes=[
            pltpu.VMEM((ROWS, D), BF),
            pltpu.VMEM((4, ROWS, 4096), BF),
            pltpu.VMEM((2, 8, 128), jnp.int32),
            pltpu.VMEM((CTX, 4, HALF, GW), BF),
            pltpu.VMEM((CTX, 4, HALF, GW), BF),
            pltpu.VMEM((CHUNKS, 2, TILES, 2, HALF, 256), BF),
            pltpu.VMEM((CHUNKS, TILES, SIDE + 1, SIDE, HALF, 256), BF),
            pltpu.VMEM((CHUNKS, 2, 2, SIDE, HALF, 256), BF),
            pltpu.VMEM((2, 2, 3 * HS, SLOTS), BF),
            pltpu.VMEM((SLOTS, 1), jnp.int32),
            pltpu.VMEM((1, SLOTS), jnp.int32),
            pltpu.VMEM((1, SLOTS), F32),
            pltpu.VMEM((HS, SLOTS), BF),
            pltpu.VMEM((HS, SLOTS), BF),
            pltpu.VMEM((SLOTS, HS), F32),
            pltpu.VMEM((SLOTS, HS), F32),
            pltpu.VMEM((2, UNITS, BLOCK, 128), BF),
            pltpu.VMEM((2, UNITS, BLOCK, 128), BF),
            pltpu.VMEM((2, 2, UNITS, BLOCK, 128), BF),
            pltpu.VMEM((2, 2, 2, 3, BLOCK, 128), BF),
            pltpu.VMEM((2, UNITS, BLOCK, 128), F32),
            pltpu.VMEM((2, 3, BLOCK, 128), BF),
            pltpu.VMEM((2, 3, BLOCK, 128), BF),
            dma((5,)),
            dma((CHUNKS,)),
            dma((3,)),
            dma((3,)),
            dma((CTX,)),
            dma((CTX,)),
            dma((CTX,)),
            dma((CTX,)),
            dma((CHUNKS, 18)),
            dma((CHUNKS, 18)),
            dma((12,)),
            dma((12,)),
        ],
        compiler_params=pltpu.CompilerParams(
            collective_id=0, has_side_effects=True, vmem_limit_bytes=62 * 2**20
        ),
    )(layer_input, query_rows, key_rows, value_rows, out_grad, doc_lengths, dilations, seg_lengths)
    wide = jax.ShapeDtypeStruct((ROWS, 4096), BF)
    out, gq, gk, gv, weight = pl.pallas_call(
        finish_kernel,
        grid=(2,),
        out_shape=(wide, wide, wide, wide, jax.ShapeDtypeStruct((3, BLOCK, GW), F32)),
        in_specs=[
            pl.BlockSpec((8, 4, HALF, GW), lambda i: (i, 0, 0, 0)),
            pl.BlockSpec((UNITS // 2, BLOCK, 128), lambda i: (i, 0, 0)),
        ],
        out_specs=[pl.BlockSpec((ROWS, 2048), lambda i: (0, i))] * 4
        + [pl.BlockSpec((3, BLOCK // 2, GW), lambda i: (0, i, 0))],
        compiler_params=pltpu.CompilerParams(vmem_limit_bytes=62 * 2**20),
    )(back, wsum)
    return out, gq, gk, gv, jnp.transpose(weight, (1, 0, 2))


def solution(mesh):
    rows = P(("dp", "ctx"), None)
    return jax.shard_map(
        on_device,
        mesh=mesh,
        in_specs=(rows, rows, rows, rows, rows, P("dp", None), P(), P()),
        out_specs=(rows, rows, rows, rows, P("dp", None, "ctx")),
        check_vma=False,
    )
```
